512 devices in a mesh: prompt: 16 (over y_lo, x, core), reply: 32 (over y_hi, z).
Axes of the slice: x: 4, y: 8 (y_hi: 4, y_lo: 2; y = y_hi * 2 + y_lo), z: 8, core: 2. Of those that a mesh axis runs over, the one named last changes fastest.
Arguments:
- q_prompt: bfloat16 [1024, 4096], P('prompt', 'reply'), may hold values from -6 to 6
- do_prompt: bfloat16 [1024, 4096], P('prompt', 'reply'), may hold values from -6 to 6
- kv_prompt: bfloat16 [2, 1024, 512], P(None, 'prompt'), may hold values from -6 to 6
- lse_prompt: float32 [32, 1024], P('reply', 'prompt')
- delta_prompt: float32 [32, 1024], P('reply', 'prompt'), may hold values from -8 to 8
- q_reply: bfloat16 [32, 1024, 4096], P('reply', 'prompt'), may hold values from -6 to 6
- do_reply: bfloat16 [32, 1024, 4096], P('reply', 'prompt'), may hold values from -6 to 6
- kv_reply: bfloat16 [2, 32, 1024, 512], P(None, 'reply', 'prompt'), may hold values from -6 to 6
- lse_reply: float32 [32, 32, 1024], P('reply', None, 'prompt')
- delta_reply: float32 [32, 32, 1024], P('reply', None, 'prompt'), may hold values from -8 to 8
- reply_len: int32 [32], P('reply'), may hold values from 256 to 1024, as said below
- reply_mask: int32 [32, 1024], P('reply', 'prompt'), may hold values 0 or 1
Outputs:
- dq_prompt: bfloat16 [1024, 4096], P('prompt', 'reply')
- dkv_prompt: bfloat16 [2, 1024, 512], P(None, 'prompt')
- dq_reply: bfloat16 [32, 1024, 4096], P('reply', 'prompt')
- dkv_reply: bfloat16 [2, 32, 1024, 512], P(None, 'reply', 'prompt')
The draws below stay inside these ranges and needn't reach their ends.
Inputs may be any that keep to these rules, and one draw needn't show every extreme that they name: `reply_len`: at least one reply fills all 1024 positions.
All inputs are finite; a program needn't handle non-finite values. No bound on the sum of `reply_mask` on one device may be relied on, other than what follows from the above.
Results may differ from the reference program's by a relative error of at most 0.005.
Values may be sent and summed in bfloat16 or wider, within the bound.
A program may use at most 64 MiB of HBM per device.

```python
import jax
import jax.numpy as jnp
from jax import lax

H = 32
G = 4
DH = 128
LP = 1024
LR = 1024
NREP = 32


def draw_lse_prompt(key, part):
    key = jax.random.fold_in(key, 11)
    places = jnp.arange(LP, dtype=jnp.float32) + 1.0
    noise = jax.random.uniform(key, (H, LP), jnp.float32, -0.3, 0.3)
    return jnp.log(places)[None, :] + 1.1 + noise


def draw_lse_reply(key, part):
    key = jax.random.fold_in(key, 12)
    places = jnp.arange(LR, dtype=jnp.float32) + 1.0 + LP
    noise = jax.random.uniform(key, (NREP, H, LR), jnp.float32, -0.3, 0.3)
    return jnp.log(places)[None, None, :] + 1.1 + noise


def draw_reply_len(key, part):
    key = jax.random.fold_in(key, 13)
    first, second = jax.random.split(key)
    lengths = jax.random.randint(first, (NREP,), LR // 4, LR + 1)
    longest = jax.random.randint(second, (), 0, NREP)
    return jnp.where(jnp.arange(NREP) == longest, LR, lengths).astype(jnp.int32)


def with_ends(values, key, smallest, largest):
    shape = values.shape
    index_at = [jax.random.randint(jax.random.fold_in(key, axis), (), 0, shape[axis]) for axis in range(len(shape))]
    values = values.at[tuple(index_at)].set(smallest)
    longest = shape.index(max(shape))
    index_at[longest] = (index_at[longest] + 1) % shape[longest]
    return values.at[tuple(index_at)].set(largest)


def block_levels(stream_key, shape, cuts, smallest, largest):
    level, own = 1.0, jax.random.fold_in(stream_key, 6)
    for position, blocks in cuts:
        draws = jnp.exp(jax.random.uniform(jax.random.fold_in(own, position), (blocks,), jnp.float32, smallest / len(cuts), largest / len(cuts)))
        level = level * jnp.repeat(draws, shape[position] // blocks).reshape([-1 if axis == position else 1 for axis in range(len(shape))])
    return level


def scatter_about(stream_key, extent, deviation, reach, pieces=(), kind=jnp.bfloat16):
    array = deviation * jax.random.normal(stream_key, extent, jnp.float32)
    if pieces:
        array = array * block_levels(stream_key, extent, pieces, -0.22, 0.18)
    return jnp.clip(array, -reach, reach).astype(kind)


def setup_inputs(seed: int = 0) -> dict:
    arg_keys = jax.random.split(jax.random.key(seed), 13)
    q_prompt = scatter_about(arg_keys[0], (LP, H * DH), 1.5, 6.0, ((0, 16), (1, 32)))
    do_prompt = scatter_about(arg_keys[1], (LP, H * DH), 1.0, 6.0, ((0, 16), (1, 32)))
    kv_prompt = scatter_about(arg_keys[2], (2, LP, G * DH), 1.0, 6.0, ((1, 16),))
    lse_prompt = draw_lse_prompt(jax.random.fold_in(arg_keys[12], 71), 0)
    delta_prompt = scatter_about(arg_keys[4], (H, LP), 2.0, 8.0, ((0, 32), (1, 16)), jnp.float32)
    q_reply = scatter_about(arg_keys[5], (NREP, LR, H * DH), 1.5, 6.0, ((0, 32), (1, 16)))
    do_reply = scatter_about(arg_keys[6], (NREP, LR, H * DH), 1.0, 6.0, ((0, 32), (1, 16)))
    kv_reply = scatter_about(arg_keys[7], (2, NREP, LR, G * DH), 1.0, 6.0, ((1, 32), (2, 16)))
    lse_reply = draw_lse_reply(jax.random.fold_in(arg_keys[12], 71), 0)
    delta_reply = scatter_about(arg_keys[9], (NREP, H, LR), 2.0, 8.0, ((0, 32), (2, 16)), jnp.float32)
    reply_len = draw_reply_len(jax.random.fold_in(arg_keys[12], 71), 0)
    reply_mask = with_ends((jax.random.randint(arg_keys[11], (NREP, LR), 0, 8) < 7).astype(jnp.int32), jax.random.fold_in(arg_keys[11], 1), 0, 1)
    return dict(q_prompt=q_prompt, do_prompt=do_prompt, kv_prompt=kv_prompt, lse_prompt=lse_prompt, delta_prompt=delta_prompt, q_reply=q_reply, do_reply=do_reply, kv_reply=kv_reply, lse_reply=lse_reply, delta_reply=delta_reply, reply_len=reply_len, reply_mask=reply_mask)


def attend(q, do, lse, delta, k, v, allow):
    f = jnp.float32
    scale = DH ** -0.5
    score = jnp.einsum('qgxd,kgd->gxqk', q.astype(f), k.astype(f)) * scale
    prob = jnp.where(allow, jnp.exp(score - lse[..., None]), 0.0)
    prob_b = prob.astype(jnp.bfloat16)
    dprob = jnp.einsum('qgxd,kgd->gxqk', do.astype(f), v.astype(f))
    dscore_b = (prob * (dprob - delta[..., None])).astype(jnp.bfloat16)
    grad_q = jnp.einsum('gxqk,kgd->qgxd', dscore_b.astype(f), k.astype(f)) * scale
    grad_k = jnp.einsum('gxqk,qgxd->kgd', dscore_b.astype(f), q.astype(f)) * scale
    grad_v = jnp.einsum('gxqk,qgxd->kgd', prob_b.astype(f), do.astype(f))
    return grad_q, grad_k, grad_v


def reference(q_prompt, do_prompt, kv_prompt, lse_prompt, delta_prompt, q_reply, do_reply, kv_reply, lse_reply, delta_reply, reply_len, reply_mask):
    group = H // G
    lp = q_prompt.shape[0]
    lr = q_reply.shape[1]
    keys_p = kv_prompt[0].reshape(lp, G, DH)
    vals_p = kv_prompt[1].reshape(lp, G, DH)
    pos_p = jnp.arange(lp, dtype=jnp.int32)
    allow_p = pos_p[None, :] <= pos_p[:, None]
    dq_p, dk_p, dv_p = attend(q_prompt.reshape(lp, G, group, DH), do_prompt.reshape(lp, G, group, DH),
                              lse_prompt.reshape(G, group, lp), delta_prompt.reshape(G, group, lp),
                              keys_p, vals_p, allow_p)
    pos_r = jnp.arange(lr, dtype=jnp.int32)

    def one_reply(carry, items):
        q_one, do_one, k_one, v_one, lse_one, delta_one, length, mask = items
        live = pos_r < length
        keys_ok = live & (mask == 1)
        allow_a = jnp.broadcast_to(live[:, None], (lr, lp))
        allow_b = (pos_r[None, :] <= pos_r[:, None]) & keys_ok[None, :] & live[:, None]
        allow = jnp.concatenate([allow_a, allow_b], axis=1)
        keys = jnp.concatenate([keys_p, k_one.reshape(lr, G, DH)], axis=0)
        vals = jnp.concatenate([vals_p, v_one.reshape(lr, G, DH)], axis=0)
        grad_q, grad_k, grad_v = attend(q_one.reshape(lr, G, group, DH), do_one.reshape(lr, G, group, DH),
                                        lse_one.reshape(G, group, lr), delta_one.reshape(G, group, lr),
                                        keys, vals, allow)
        carry = (carry[0] + grad_k[:lp], carry[1] + grad_v[:lp])
        return carry, (grad_q.reshape(lr, H * DH), grad_k[lp:].reshape(lr, G * DH), grad_v[lp:].reshape(lr, G * DH))

    (dk_all, dv_all), (dq_r, dk_r, dv_r) = lax.scan(
        one_reply, (dk_p, dv_p),
        (q_reply, do_reply, kv_reply[0], kv_reply[1], lse_reply, delta_reply, reply_len, reply_mask))
    dq_prompt = dq_p.reshape(lp, H * DH).astype(jnp.bfloat16)
    dkv_prompt = jnp.stack([dk_all, dv_all]).reshape(2, lp, G * DH).astype(jnp.bfloat16)
    dkv_reply = jnp.stack([dk_r, dv_r]).astype(jnp.bfloat16)
    return dq_prompt, dkv_prompt, dq_r.astype(jnp.bfloat16), dkv_reply
```

```python
import jax
import jax.numpy as jnp
from jax import lax
from jax.experimental import pallas as pl
from jax.experimental.pallas import tpu as pltpu
from jax.sharding import PartitionSpec as P

MESH = pl.DeviceIdType.MESH
F32 = jnp.float32
BF16 = jnp.bfloat16
DH = 128
NP = 16
NR = 32
ROWS = 64
CHIP = 2 * ROWS
UNIT = 256
SCALE = DH**-0.5
LOG2E = 1.4426950408889634
NT = (((1,), (1,)), ((), ()))
TN = (((0,), (0,)), ((), ()))


def dot(a, b, dims=(((1,), (0,)), ((), ()))):
    return lax.dot_general(a, b, dims, preferred_element_type=F32)


def kernel(
    qp, dop, kvp, lsep, delp, qr, dor, kvr, lser, delr, rlen, rmask,
    dqp_out, dkvp_out, dqr_out, dkvr_out,
    qbuf, dobuf, qpb, dopb, kpb, krb, lsd_st, lsd_rx, lsp_st, lsp_rx, msk_st, msk_rx,
    lse2, del2, rows_p, bias, dqa, dqpa, dacc, psend, prx, rsend, rrx, rs_st, rs_rx, ag_st, dq_st, dqp_st,
    loc, ex_s, ex_r, kps, kpr, krs, krr, mks, mkr, pps, ppr, rps, rpr, rss, rsr, ags, agr, out_s, out_r,
):
    p = lax.axis_index("prompt")
    r = lax.axis_index("reply")
    k = p % 2
    u = p // 2
    m = p // 4
    sib = p + 1 - 2 * k
    handler = r // 16
    hgroup = (r // 8) % 2
    mine = pl.ds(pl.multiple_of(64 * k, 64), ROWS)
    other = pl.ds(pl.multiple_of(64 * (1 - k), 64), ROWS)
    my_cols = pl.ds(pl.multiple_of(2048 * k, 2048), 2048)
    sib_cols = pl.ds(pl.multiple_of(2048 * (1 - k), 2048), 2048)

    def remote(src, dst, send, recv, **where):
        return pltpu.make_async_remote_copy(
            src_ref=src, dst_ref=dst, send_sem=send, recv_sem=recv, device_id=where, device_id_type=MESH
        )

    barrier = pltpu.get_barrier_semaphore()

    @pl.loop(1, NP)
    def _(o):
        pl.semaphore_signal(barrier, inc=1, device_id={"prompt": (p + o) % NP}, device_id_type=MESH)

    @pl.loop(1, NR)
    def _(o):
        pl.semaphore_signal(barrier, inc=1, device_id={"reply": (r + o) % NR}, device_id_type=MESH)

    def kv_piece(ref, core):
        return ref.at[:, :, pl.ds(pl.multiple_of(256 * core, 256), 256)]

    def rows_of(ref, q):
        return ref.at[:, pl.ds(pl.multiple_of(ROWS * q, ROWS), ROWS), :]

    local = [
        pltpu.make_async_copy(qr.at[0, :, my_cols], qbuf.at[mine, :], loc.at[0]),
        pltpu.make_async_copy(dor.at[0, :, my_cols], dobuf.at[mine, :], loc.at[1]),
        pltpu.make_async_copy(kv_piece(kvp, k), rows_of(kpb, p), loc.at[2]),
        pltpu.make_async_copy(kv_piece(kvr.at[:, 0], k), rows_of(krb, p), loc.at[3]),
        pltpu.make_async_copy(qp, qpb.at[mine, :], loc.at[4]),
        pltpu.make_async_copy(dop, dopb.at[mine, :], loc.at[5]),
    ]
    for copy in local:
        copy.start()

    def twice(x):
        return jnp.concatenate([x, x], axis=1)

    def heads_of(ref, core):
        return twice(ref[0, pl.ds(pl.multiple_of(16 * core, 16), 16), :])

    lsd_st[0] = heads_of(lser, 1 - k)
    lsd_st[1] = heads_of(delr, 1 - k)
    lsp_st[0:1, :] = twice(lsep[...])
    lsp_st[1:2, :] = twice(delp[...])
    lsp_st[2:8, :] = jnp.zeros((6, 128), F32)
    msk_st[...] = jnp.broadcast_to(twice(rmask[...].astype(F32)), (8, 128))

    pl.semaphore_wait(barrier, NP - 1 + NR - 1)

    exchange = [
        remote(qr.at[0, :, sib_cols], qbuf.at[mine, :], ex_s.at[0], ex_r.at[0], prompt=sib),
        remote(dor.at[0, :, sib_cols], dobuf.at[mine, :], ex_s.at[1], ex_r.at[1], prompt=sib),
        remote(lsd_st, lsd_rx, ex_s.at[2], ex_r.at[2], prompt=sib),
        remote(qp, qpb.at[mine, :], ex_s.at[3], ex_r.at[3], prompt=sib),
        remote(dop, dopb.at[mine, :], ex_s.at[4], ex_r.at[4], prompt=sib),
        remote(lsp_st, lsp_rx, ex_s.at[5], ex_r.at[5], prompt=sib),
    ]
    arrivals = [
        remote(qr.at[0, :, sib_cols], qbuf.at[other, :], ex_s.at[0], ex_r.at[0], prompt=sib),
        remote(dor.at[0, :, sib_cols], dobuf.at[other, :], ex_s.at[1], ex_r.at[1], prompt=sib),
        remote(lsd_st, lsd_rx, ex_s.at[2], ex_r.at[2], prompt=sib),
        remote(qp, qpb.at[other, :], ex_s.at[3], ex_r.at[3], prompt=sib),
        remote(dop, dopb.at[other, :], ex_s.at[4], ex_r.at[4], prompt=sib),
        remote(lsp_st, lsp_rx, ex_s.at[5], ex_r.at[5], prompt=sib),
    ]
    for copy in exchange:
        copy.start()

    def kp_copy(src_p, dst_p):
        return remote(kv_piece(kvp, dst_p % 2), rows_of(kpb, src_p), kps.at[dst_p], kpr.at[src_p], prompt=dst_p)

    def kr_copy(src_p, dst_p):
        return remote(kv_piece(kvr.at[:, 0], dst_p % 2), rows_of(krb, src_p), krs.at[dst_p], krr.at[src_p], prompt=dst_p)

    def mk_copy(src_p, dst_p):
        return remote(msk_st, msk_rx.at[src_p], mks.at[dst_p], mkr.at[src_p], prompt=dst_p)

    @pl.loop(1, NP)
    def _(o):
        kp_copy(p, (p + NP - o) % NP).start()

    @pl.loop(1, NP)
    def _(o):
        peer = (p + NP - o) % NP

        @pl.when(peer // 4 >= m)
        def _():
            mk_copy(p, peer).start()
            kr_copy(p, peer).start()

    msk_rx[p] = msk_st[...]
    dqa[...] = jnp.zeros_like(dqa)
    dqpa[...] = jnp.zeros_like(dqpa)

    local[0].wait()
    local[1].wait()
    local[4].wait()
    local[5].wait()
    for copy in arrivals:
        copy.wait_recv()

    lane = lax.broadcasted_iota(jnp.int32, (1, 128), 1)
    first = lane < 64
    own = first == (k == 0)
    qpos = CHIP * u + lane
    alive = qpos < rlen[0]
    lse_all = jnp.where(own, heads_of(lser, k), lsd_rx[0]) * LOG2E
    lse_all = jnp.where(alive, lse_all, jnp.inf)
    del_all = jnp.where(own, heads_of(delr, k), lsd_rx[1])
    for g in range(2):
        for hp in range(4):
            h = 8 * g + 2 * hp
            lse2[g, hp:hp + 1, :] = jnp.concatenate([lse_all[h:h + 1], lse_all[h + 1:h + 2]], axis=1)
            del2[g, hp:hp + 1, :] = jnp.concatenate([del_all[h:h + 1], del_all[h + 1:h + 2]], axis=1)
    rows_p[0:1, :] = jnp.where(own, lsp_st[0:1, :], lsp_rx[0:1, :]) * LOG2E
    rows_p[1:2, :] = jnp.where(own, lsp_st[1:2, :], lsp_rx[1:2, :])

    def terms(keys, vals, q, do, lse_row, del_row, add):
        score = dot(keys, q, NT) * (SCALE * LOG2E) - lse_row
        if add is not None:
            score = score + add
        prob = jnp.exp2(score)
        dprob = dot(vals, do, NT)
        prob_b = prob.astype(BF16)
        ds_b = (prob * (dprob - del_row)).astype(BF16)
        return dot(ds_b, keys, TN), dot(ds_b, q), dot(prob_b, do)

    def unit(ref, s, masked):
        rows = pl.ds(pl.multiple_of(UNIT * s, UNIT), UNIT)

        @pl.loop(0, 2)
        def _(g):
            cols = pl.ds(pl.multiple_of(DH * g, DH), DH)
            keys = ref[0, rows, cols]
            vals = ref[1, rows, cols]
            dk = dv = None
            for hp in range(4):
                c0 = pl.ds(pl.multiple_of(1024 * g + 256 * hp, 128), 128)
                c1 = pl.ds(pl.multiple_of(1024 * g + 256 * hp + 128, 128), 128)
                q = jnp.concatenate([qbuf[:, c0], qbuf[:, c1]], axis=0)
                do = jnp.concatenate([dobuf[:, c0], dobuf[:, c1]], axis=0)
                add = jnp.concatenate([bias[...], bias[...]], axis=1) if masked else None
                dq, dk1, dv1 = terms(
                    keys, vals, q, do, lse2[g, hp:hp + 1, :], del2[g, hp:hp + 1, :], add
                )
                dqa[4 * g + hp] += dq
                dk = dk1 if dk is None else dk + dk1
                dv = dv1 if dv is None else dv + dv1
            dacc[0, g] = dk
            dacc[1, g] = dv

    def store_partial(buf, s):
        for g in range(2):
            cols = slice(DH * g, DH * g + DH)
            buf[s, 0, :, cols] = (dacc[0, g] * SCALE).astype(BF16)
            buf[s, 1, :, cols] = dacc[1, g].astype(BF16)

    def partial_own(buf, rx, sem, s, j):
        return pltpu.make_async_copy(buf.at[s, :, pl.ds(pl.multiple_of(ROWS * j, ROWS), ROWS), :], rx.at[p], sem.at[p])

    def partial_copy(buf, rx, send, recv, src_p, dst_p):
        src = buf.at[dst_p // 4, :, pl.ds(pl.multiple_of(ROWS * (dst_p % 4), ROWS), ROWS), :]
        return remote(src, rx.at[src_p], send.at[dst_p], recv.at[src_p], prompt=dst_p)

    def send_partial(buf, rx, send, recv, s):
        @pl.loop(0, 4)
        def _(j):
            dst_p = 4 * s + j

            @pl.when(dst_p == p)
            def _():
                partial_own(buf, rx, recv, s, j).start()

            @pl.when(dst_p != p)
            def _():
                partial_copy(buf, rx, send, recv, p, dst_p).start()

    def wait_partial(buf, rx, send, recv, src_p):
        @pl.when(src_p == p)
        def _():
            partial_own(buf, rx, recv, m, p % 4).wait()

        @pl.when(src_p != p)
        def _():
            partial_copy(buf, rx, send, recv, src_p, p).wait_recv()

    def sum_partials(rx, lo, core):
        def add(v, acc):
            return acc + rx[2 * v + core].astype(F32)

        return lax.fori_loop(lo, NP // 2, add, jnp.zeros((2, ROWS, 2 * DH), F32))

    @pl.loop(0, 4)
    def _(i):
        s = (m + i) % 4

        @pl.loop(0, 4)
        def _(j):
            src_p = 4 * s + j

            @pl.when(src_p == p)
            def _():
                local[2].wait()

            @pl.when(src_p != p)
            def _():
                kp_copy(src_p, p).wait_recv()

        unit(kpb, s, False)

        @pl.when((k == handler) & (s <= m))
        def _():
            rows = pl.ds(pl.multiple_of(UNIT * s, UNIT), UNIT)
            cols = pl.ds(pl.multiple_of(DH * hgroup, DH), DH)
            key_row = lax.broadcasted_iota(jnp.int32, (UNIT, CHIP), 0)
            query = lax.broadcasted_iota(jnp.int32, (UNIT, CHIP), 1)
            add = jnp.where(key_row - query <= CHIP * u - UNIT * s, 0.0, -jnp.inf)
            dq, dk, dv = terms(
                kpb[0, rows, cols], kpb[1, rows, cols], qpb[...], dopb[...], rows_p[0:1, :], rows_p[1:2, :], add
            )
            dqpa[...] += dq
            dacc[0, hgroup] += dk
            dacc[1, hgroup] += dv

        store_partial(psend, s)
        send_partial(psend, prx, pps, ppr, s)

    dqp_st[...] = (dqpa[...] * SCALE).astype(BF16)
    dqp_own = pltpu.make_async_copy(dqp_st.at[mine, :], dqp_out, loc.at[4])
    dqp_send = remote(dqp_st.at[other, :], dqp_out, out_s.at[0], out_r.at[0], prompt=sib)

    @pl.when(k == handler)
    def _():
        dqp_own.start()
        dqp_send.start()

    def rs_copy(src_r, dst_r):
        return remote(rs_st.at[dst_r], rs_rx.at[src_r], rss.at[dst_r], rsr.at[src_r], reply=dst_r)

    def piece(ref, i):
        a, b = i // 4, i % 4
        return ref.at[a // 4, pl.ds(pl.multiple_of(16 * (a % 4), 16), 16), pl.ds(pl.multiple_of(DH * b, DH), DH)]

    def ag_copy(src_r, dst_r):
        return remote(ag_st, piece(dkvp_out, src_r), ags.at[dst_r], agr.at[src_r], reply=dst_r)

    ag_own = pltpu.make_async_copy(ag_st, piece(dkvp_out, r), loc.at[6])

    def reduce_start():
        @pl.loop(0, NP)
        def _(src_p):
            wait_partial(psend, prx, pps, ppr, src_p)

        for core in range(2):
            total = sum_partials(prx, 0, core).astype(BF16)
            for kv in range(2):
                for chunk in range(4):
                    for half in range(2):
                        i = (kv * 4 + chunk) * 4 + 2 * core + half
                        rs_st[i] = total[kv, 16 * chunk:16 * chunk + 16, DH * half:DH * half + DH]
        rs_rx[r] = rs_st[r]

        @pl.loop(1, NR)
        def _(o):
            rs_copy(r, (r + o) % NR).start()

    def reduce_finish():
        @pl.loop(1, NR)
        def _(o):
            rs_copy((r + o) % NR, r).wait_recv()

        total = lax.fori_loop(0, NR, lambda i, acc: acc + rs_rx[i].astype(F32), jnp.zeros((16, DH), F32))
        ag_st[...] = total.astype(BF16)
        ag_own.start()

        @pl.loop(1, NR)
        def _(o):
            ag_copy(r, (r + o) % NR).start()

    @pl.loop(0, m + 1)
    def _(s):
        @pl.loop(0, 4)
        def _(j):
            src_p = 4 * s + j

            @pl.when(src_p == p)
            def _():
                local[3].wait()

            @pl.when(src_p != p)
            def _():
                kr_copy(src_p, p).wait_recv()
                mk_copy(src_p, p).wait_recv()

        key_row = lax.broadcasted_iota(jnp.int32, (CHIP, CHIP), 0)
        query = lax.broadcasted_iota(jnp.int32, (CHIP, CHIP), 1)
        for half in range(2):
            row = jnp.where(first, msk_rx[4 * s + 2 * half, 0:1, :], msk_rx[4 * s + 2 * half + 1, 0:1, :])
            column = jnp.transpose(jnp.broadcast_to(row, (CHIP, CHIP)))
            ok = (key_row - query <= CHIP * u - UNIT * s - CHIP * half) & (column > 0.5)
            bias[CHIP * half:CHIP * half + CHIP, :] = jnp.where(ok, 0.0, -jnp.inf)
        unit(krb, s, True)
        store_partial(rsend, s)
        send_partial(rsend, rrx, rps, rpr, s)

        @pl.when(s == 0)
        def _():
            reduce_start()

        @pl.when(s == jnp.minimum(m, 2))
        def _():
            reduce_finish()

    for hp in range(8):
        part = (dqa[hp] * SCALE).astype(BF16)
        dq_st[:, 256 * hp:256 * hp + 128] = part[0:128]
        dq_st[:, 256 * hp + 128:256 * hp + 256] = part[128:256]
    dq_send = remote(dq_st.at[other, :], dqr_out.at[0, :, my_cols], out_s.at[1], out_r.at[1], prompt=sib)
    dq_recv = remote(dq_st.at[other, :], dqr_out.at[0, :, sib_cols], out_s.at[1], out_r.at[1], prompt=sib)
    dq_own = pltpu.make_async_copy(dq_st.at[mine, :], dqr_out.at[0, :, my_cols], loc.at[0])
    dq_send.start()
    dq_own.start()

    @pl.loop(4 * m, NP)
    def _(src_p):
        wait_partial(rsend, rrx, rps, rpr, src_p)

    for core in range(2):
        dkvr_out[:, 0, :, 2 * DH * core:2 * DH * core + 2 * DH] = sum_partials(rrx, 2 * m, core).astype(BF16)

    @pl.loop(1, NR)
    def _(o):
        ag_copy((r + o) % NR, r).wait_recv()

    ag_own.wait()
    dq_own.wait()
    dq_recv.wait_recv()

    @pl.when(k == handler)
    def _():
        dqp_own.wait()
        dqp_send.wait_send()

    @pl.when(k != handler)
    def _():
        dqp_send.wait_recv()

    dq_send.wait_send()
    for copy in exchange:
        copy.wait_send()

    @pl.loop(1, NP)
    def _(o):
        peer = (p + o) % NP
        kp_copy(p, peer).wait_send()
        partial_copy(psend, prx, pps, ppr, p, peer).wait_send()

        @pl.when(peer // 4 >= m)
        def _():
            mk_copy(p, peer).wait_send()
            kr_copy(p, peer).wait_send()

        @pl.when(peer // 4 <= m)
        def _():
            partial_copy(rsend, rrx, rps, rpr, p, peer).wait_send()

    @pl.loop(1, NR)
    def _(o):
        peer = (r + o) % NR
        rs_copy(r, peer).wait_send()
        ag_copy(r, peer).wait_send()


def call(*args):
    anywhere = pl.BlockSpec(memory_space=pl.ANY)
    vmem = pl.BlockSpec(memory_space=pltpu.VMEM)
    smem = pl.BlockSpec(memory_space=pltpu.SMEM)
    dma = pltpu.SemaphoreType.DMA
    out = jax.ShapeDtypeStruct
    return pl.pallas_call(
        kernel,
        out_shape=(
            out((ROWS, DH), BF16),
            out((2, ROWS, 512), BF16),
            out((1, ROWS, 4096), BF16),
            out((2, 1, ROWS, 512), BF16),
        ),
        in_specs=[
            anywhere, anywhere, anywhere, vmem, vmem, anywhere, anywhere, anywhere, vmem, vmem, smem, vmem,
        ],
        out_specs=(anywhere, anywhere, anywhere, vmem),
        scratch_shapes=[
            pltpu.VMEM((CHIP, 2048), BF16),
            pltpu.VMEM((CHIP, 2048), BF16),
            pltpu.VMEM((CHIP, DH), BF16),
            pltpu.VMEM((CHIP, DH), BF16),
            pltpu.VMEM((2, 1024, 256), BF16),
            pltpu.VMEM((2, 1024, 256), BF16),
            pltpu.VMEM((2, 16, 128), F32),
            pltpu.VMEM((2, 16, 128), F32),
            pltpu.VMEM((8, 128), F32),
            pltpu.VMEM((8, 128), F32),
            pltpu.VMEM((8, 128), F32),
            pltpu.VMEM((NP, 8, 128), F32),
            pltpu.VMEM((2, 4, 256), F32),
            pltpu.VMEM((2, 4, 256), F32),
            pltpu.VMEM((8, 128), F32),
            pltpu.VMEM((UNIT, CHIP), F32),
            pltpu.VMEM((8, 256, DH), F32),
            pltpu.VMEM((CHIP, DH), F32),
            pltpu.VMEM((2, 2, UNIT, DH), F32),
            pltpu.VMEM((4, 2, UNIT, 256), BF16),
            pltpu.VMEM((NP, 2, ROWS, 256), BF16),
            pltpu.VMEM((4, 2, UNIT, 256), BF16),
            pltpu.VMEM((NP, 2, ROWS, 256), BF16),
            pltpu.VMEM((NR, 16, DH), BF16),
            pltpu.VMEM((NR, 16, DH), BF16),
            pltpu.VMEM((16, DH), BF16),
            pltpu.VMEM((CHIP, 2048), BF16),
            pltpu.VMEM((CHIP, DH), BF16),
            dma((7,)),
            dma((6,)),
            dma((6,)),
            dma((NP,)),
            dma((NP,)),
            dma((NP,)),
            dma((NP,)),
            dma((NP,)),
            dma((NP,)),
            dma((NP,)),
            dma((NP,)),
            dma((NP,)),
            dma((NP,)),
            dma((NR,)),
            dma((NR,)),
            dma((NR,)),
            dma((NR,)),
            dma((2,)),
            dma((2,)),
        ],
        compiler_params=pltpu.CompilerParams(
            collective_id=0, has_side_effects=True, vmem_limit_bytes=48 * 2**20
        ),
    )(*args)


def solution(mesh):
    placed = (
        P("prompt", "reply"),
        P("prompt", "reply"),
        P(None, "prompt", None),
        P("reply", "prompt"),
        P("reply", "prompt"),
        P("reply", "prompt", None),
        P("reply", "prompt", None),
        P(None, "reply", "prompt", None),
        P("reply", None, "prompt"),
        P("reply", None, "prompt"),
        P("reply"),
        P("reply", "prompt"),
    )
    return jax.shard_map(
        call,
        mesh=mesh,
        in_specs=placed,
        out_specs=(
            P("prompt", "reply"),
            P(None, "prompt", None),
            P("reply", "prompt", None),
            P(None, "reply", "prompt", None),
        ),
        check_vma=False,
    )
```

```python
import jax
import jax.numpy as jnp
from jax import lax
from jax.experimental import pallas as pl
from jax.experimental.pallas import tpu as pltpu
from jax.sharding import PartitionSpec as P

MESH = pl.DeviceIdType.MESH
F32 = jnp.float32
BF16 = jnp.bfloat16
DH = 128
ROWS = 64
HALF = 128
UNIT = 256
WIDE = 1024
SCALE = DH**-0.5
LOG2E = 1.4426950408889634
NN = (((1,), (0,)), ((), ()))
NT = (((1,), (1,)), ((), ()))
TN = (((0,), (0,)), ((), ()))


def dot(a, b, dims=NN):
    return lax.dot_general(a, b, dims, preferred_element_type=F32)


def at(start, size, step):
    return pl.ds(pl.multiple_of(start, step), size)


def kernel(
    qp, dop, kvp, lsep, delp, qr, dor, kvr, lser, delr, rlen, rmask,
    dqp_out, dkvp_out, dqr_out, dkvr_out,
    qbuf, dobuf, qpb, dopb, kpb, krb, lsd_st, lsd_rx, lsp_rx, msk, lse2, del2, rows_p, bias,
    dqa, dqpa, dacc, keep, psend, prx, rsend, rrx, rst, rrcv, ag_st, dq_st, dqp_st, dkv_st,
    loc, qs, qrx, ds, drx, ls, lrx, ps, prs, kp1s, kp1r, kr1s, kr1r, ms1, mr1, kp2s, kp2r, kr2s, kr2r, ms2, mr2,
    pps, ppr, rps, rpr, rss, rsr, ags, agr, os_, or_, fs, fr, dps, dpr,
):
    p = lax.axis_index("prompt")
    r = lax.axis_index("reply")
    y = p // 8
    x = (p // 2) % 4
    c = p % 2
    g = 2 * y + c
    yh = r // 8
    z = r % 8
    handler = r // 8
    turn = (r // 4) % 4
    beyond = 8 * ((yh + 2 * y + 3) % 4) + z
    near = 2 * y + 1 - c

    def device(i, j):
        return 8 * (j // 2) + 2 * i + j % 2

    def mate(j):
        return device(x, j)

    def along(i):
        return 8 * y + 2 * i + c

    def remote(src, dst, send, recv, **where):
        return pltpu.make_async_remote_copy(
            src_ref=src, dst_ref=dst, send_sem=send, recv_sem=recv, device_id=where, device_id_type=MESH
        )

    barrier = pltpu.get_barrier_semaphore()

    def greet(**where):
        pl.semaphore_signal(barrier, inc=1, device_id=where, device_id_type=MESH)

    @pl.loop(1, 4)
    def _(o):
        greet(prompt=mate((g + o) % 4))
        greet(prompt=along((x + o) % 4))

    @pl.loop(0, 2)
    def _(b):
        greet(prompt=mate(2 * (1 - y) + b), reply=beyond)

    @pl.loop(1, 32)
    def _(o):
        greet(reply=(r + o) % 32)

    def giver(i):
        return 16 * (i // 4) + 4 * g + i % 4

    @pl.loop(1, 4)
    def _(o):
        @pl.loop(0, 8)
        def _(i):
            greet(prompt=mate((g + o) % 4), reply=giver(i))

    def group_cols(j):
        return at(DH * j, DH, DH)

    def head_cols(j):
        return at(WIDE * j, WIDE, WIDE)

    def seat(ref, j):
        return ref.at[j // 2, at(ROWS * (j % 2), ROWS, ROWS), :]

    def rows_at(ref, i, j):
        return ref.at[:, at(UNIT * i + ROWS * j, ROWS, ROWS), :]

    def unit_at(ref, i):
        return ref.at[:, at(UNIT * i, UNIT, UNIT), :]

    own_kp = pltpu.make_async_copy(kvp.at[:, :, group_cols(g)], rows_at(kpb, x, g), loc.at[2])
    own_kr = pltpu.make_async_copy(kvr.at[:, 0, :, group_cols(g)], rows_at(krb, x, g), loc.at[3])
    own_q = pltpu.make_async_copy(qr.at[0, :, head_cols(g)], seat(qbuf, g), loc.at[0])
    own_do = pltpu.make_async_copy(dor.at[0, :, head_cols(g)], seat(dobuf, g), loc.at[1])
    own_qp = pltpu.make_async_copy(qp, seat(qpb, g), loc.at[4])
    own_dop = pltpu.make_async_copy(dop, seat(dopb, g), loc.at[5])
    for copy in (own_kp, own_q, own_do, own_kr, own_qp, own_dop):
        copy.start()

    def twice(v):
        return jnp.concatenate([v, v], axis=1)

    for j in range(4):
        lsd_st[j, 0] = twice(lser[0, 8 * j:8 * j + 8, :])
        lsd_st[j, 1] = twice(delr[0, 8 * j:8 * j + 8, :])
    lsp_rx[g, 0:1, :] = twice(lsep[...])
    lsp_rx[g, 1:2, :] = twice(delp[...])
    lsp_rx[g, 2:8, :] = jnp.zeros((6, 128), F32)
    msk[x, g] = jnp.broadcast_to(twice(rmask[...].astype(F32)), (8, 128))
    lsd_rx[g] = lsd_st[g]

    @pl.when(turn == g)
    def _():
        pl.semaphore_wait(barrier, 3 + 3 + 2 + 31)

    @pl.when(turn != g)
    def _():
        pl.semaphore_wait(barrier, 3 + 3 + 2 + 31 + 32)

    def kp1(src, dst, **where):
        piece = kvp.at[:, :, group_cols(dst)]
        return remote(piece, rows_at(kpb, x, src), kp1s.at[dst], kp1r.at[src], prompt=mate(dst), **where)

    def kr1(src, dst):
        return remote(kvr.at[:, 0, :, group_cols(dst)], rows_at(krb, x, src), kr1s.at[dst], kr1r.at[src], prompt=mate(dst))

    def mk1(src, dst):
        return remote(msk.at[x, src], msk.at[x, src], ms1.at[dst], mr1.at[src], prompt=mate(dst))

    def chunk(ref, j, ch):
        return ref.at[j // 2, at(ROWS * (j % 2), ROWS, ROWS), at(512 * ch, 512, 512)]

    def q1(src, dst, ch):
        piece = qr.at[0, :, at(WIDE * dst + 512 * ch, 512, 512)]
        return remote(piece, chunk(qbuf, src, ch), qs.at[dst, ch], qrx.at[src, ch], prompt=mate(dst))

    def do1(src, dst, ch):
        piece = dor.at[0, :, at(WIDE * dst + 512 * ch, 512, 512)]
        return remote(piece, chunk(dobuf, src, ch), ds.at[dst, ch], drx.at[src, ch], prompt=mate(dst))

    def ls1(src, dst):
        return remote(lsd_st.at[dst], lsd_rx.at[src], ls.at[dst], lrx.at[src], prompt=mate(dst))

    def hand(src):
        return [
            remote(qp, seat(qpb, src), ps.at[0], prs.at[0, src], prompt=mate(handler)),
            remote(dop, seat(dopb, src), ps.at[1], prs.at[1, src], prompt=mate(handler)),
            remote(lsp_rx.at[src], lsp_rx.at[src], ps.at[2], prs.at[2, src], prompt=mate(handler)),
        ]

    @pl.loop(0, 2)
    def _(b):
        kp1(g, 2 * (1 - y) + (c + b) % 2, reply=beyond).start()

    kp1(g, near).start()

    ls1(g, near).start()
    for ch in range(2):
        q1(g, near, ch).start()
        do1(g, near, ch).start()

    @pl.loop(0, 2)
    def _(b):
        far = 2 * (1 - y) + (c + b) % 2
        ls1(g, far).start()
        kr1(g, far).start()
        mk1(g, far).start()

    kr1(g, near).start()
    mk1(g, near).start()

    @pl.when(g != handler)
    def _():
        for copy in hand(g):
            copy.start()

    @pl.loop(0, 4)
    def _(b):
        far = 2 * (1 - y) + (c + b) % 2
        q1(g, far, b // 2).start()
        do1(g, far, b // 2).start()

    def kp2(src, dst):
        return remote(unit_at(kpb, src), unit_at(kpb, src), kp2s.at[dst], kp2r.at[src], prompt=along(dst))

    def kr2(src, dst):
        return remote(unit_at(krb, src), unit_at(krb, src), kr2s.at[dst], kr2r.at[src], prompt=along(dst))

    def mk2(src, dst):
        return remote(msk.at[src], msk.at[src], ms2.at[dst], mr2.at[src], prompt=along(dst))

    own_kp.wait()

    @pl.loop(1, 4)
    def _(o):
        kp1((g + o) % 4, g).wait_recv()

    @pl.loop(1, 4)
    def _(o):
        kp2(x, (x + 4 - o) % 4).start()

    dqa[...] = jnp.zeros_like(dqa)
    dacc[...] = jnp.zeros_like(dacc)

    def pass_reply_keys():
        own_kr.wait()

        @pl.loop(1, 4)
        def _(o):
            kr1((g + o) % 4, g).wait_recv()
            mk1((g + o) % 4, g).wait_recv()

        @pl.loop(1, 4)
        def _(o):
            kr2(x, (x + 4 - o) % 4).start()
            mk2(x, (x + 4 - o) % 4).start()

    pass_reply_keys()

    lane = lax.broadcasted_iota(jnp.int32, (1, 128), 1)
    first = lane < 64

    def rows_of(half):
        alive = HALF * x + 512 * half + lane < rlen[0]
        lse = jnp.where(first, lsd_rx[2 * half, 0], lsd_rx[2 * half + 1, 0]) * LOG2E
        lse = jnp.where(alive, lse, jnp.inf)
        delta = jnp.where(first, lsd_rx[2 * half, 1], lsd_rx[2 * half + 1, 1])
        for ch in range(2):
            lse2[half, ch] = jnp.concatenate([lse[h:h + 1] for h in range(4 * ch, 4 * ch + 4)], axis=1)
            del2[half, ch] = jnp.concatenate([delta[h:h + 1] for h in range(4 * ch, 4 * ch + 4)], axis=1)

    own_q.wait()
    own_do.wait()
    for ch in range(2):
        q1(near, g, ch).wait_recv()
        do1(near, g, ch).wait_recv()
    ls1(near, g).wait_recv()
    rows_of(y)

    def heads(ref, half):
        return jnp.concatenate([ref[half, :, DH * h:DH * h + DH] for h in range(8)], axis=0)

    def terms(keys, vals, q, do, lse_row, del_row, add):
        score = dot(keys, q, NT) * (SCALE * LOG2E) - lse_row
        if add is not None:
            score = score + add
        prob = jnp.exp2(score)
        dprob = dot(vals, do, NT)
        prob_b = prob.astype(BF16)
        ds_b = (prob * (dprob - del_row)).astype(BF16)
        return dot(ds_b, keys, TN), dot(ds_b, q), dot(prob_b, do)

    def both(ref, half):
        return jnp.concatenate([ref[half, 0], ref[half, 1]], axis=1)

    def unit(ref, i, half, size, masked):
        rows = at(UNIT * i, size, UNIT)
        add = None
        if masked:
            add = jnp.concatenate([bias[0:size, :]] * 8, axis=1)
        dq, dk, dv = terms(
            ref[0, rows, :], ref[1, rows, :], heads(qbuf, half), heads(dobuf, half), both(lse2, half), both(del2, half), add
        )
        dqa[half] += dq
        dacc[i, 0, 0:size, :] += dk
        dacc[i, 1, 0:size, :] += dv

    def four(ref, half, ch):
        return jnp.concatenate([ref[half, :, at(512 * ch + DH * h, DH, DH)] for h in range(4)], axis=0)

    def unit_chunk(ref, i, half, ch):
        rows = at(UNIT * i, UNIT, UNIT)
        dq, dk, dv = terms(
            ref[0, rows, :], ref[1, rows, :], four(qbuf, half, ch), four(dobuf, half, ch), lse2[half, ch], del2[half, ch], None
        )
        dqa[half, at(512 * ch, 512, 512), :] += dq
        dacc[i, 0] += dk
        dacc[i, 1] += dv

    def causal(i, half, size):
        key = lax.broadcasted_iota(jnp.int32, (HALF, HALF), 0)
        query = lax.broadcasted_iota(jnp.int32, (HALF, HALF), 1)
        return [key - query <= HALF * x + 512 * half - HALF * i - 512 * b for b in range(size // HALF)]

    def set_bias(i, half, size):
        for b, ok in enumerate(causal(i, half, size)):
            row = jnp.where(first, msk[i, 2 * b, 0:1, :], msk[i, 2 * b + 1, 0:1, :])
            column = jnp.transpose(jnp.broadcast_to(row, (HALF, HALF)))
            bias[HALF * b:HALF * b + HALF, :] = jnp.where(ok & (column > 0.5), 0.0, -jnp.inf)

    def partial(buf, rx, send, recv, src, dst):
        return remote(buf.at[dst], rx.at[src], send.at[dst], recv.at[src], prompt=along(dst))

    def finish(buf, rx, send, recv, i):
        @pl.when(i == x)
        def _():
            keep[0] = dacc[x, 0] * SCALE
            keep[1] = dacc[x, 1]

        @pl.when(i != x)
        def _():
            buf[i, 0] = (dacc[i, 0] * SCALE).astype(BF16)
            buf[i, 1] = dacc[i, 1].astype(BF16)
            partial(buf, rx, send, recv, x, i).start()

    def totals_of(buf, rx, send, recv):
        @pl.loop(1, 4)
        def _(o):
            partial(buf, rx, send, recv, (x + o) % 4, x).wait_recv()

        totals = []
        for kv in range(2):
            total = keep[kv]
            for o in range(1, 4):
                total = total + rx[(x + o) % 4, kv].astype(F32)
            totals.append(total.astype(BF16))
        return totals

    @pl.loop(0, 4)
    def _(t):
        i = (x + t) % 4

        @pl.when(t > 0)
        def _():
            kp2(i, x).wait_recv()

        unit(kpb, i, y, UNIT, False)

    @pl.loop(0, 2)
    def _(b):
        ls1(2 * (1 - y) + b, g).wait_recv()

    rows_of(1 - y)

    @pl.when(g == handler)
    def _():
        own_qp.wait()
        own_dop.wait()

        @pl.loop(1, 4)
        def _(o):
            for copy in hand((g + o) % 4):
                copy.wait_recv()

        for b in range(2):
            lse = jnp.where(first, lsp_rx[2 * b, 0:1, :], lsp_rx[2 * b + 1, 0:1, :]) * LOG2E
            delta = jnp.where(first, lsp_rx[2 * b, 1:2, :], lsp_rx[2 * b + 1, 1:2, :])
            rows_p[0:1, DH * b:DH * b + DH] = lse
            rows_p[1:2, DH * b:DH * b + DH] = delta
        dqpa[...] = jnp.zeros_like(dqpa)

        @pl.loop(0, 4)
        def _(i):
            rows = at(UNIT * i, UNIT, UNIT)
            grid = [jnp.concatenate(causal(i, b, UNIT), axis=0) for b in range(2)]
            add = jnp.where(jnp.concatenate(grid, axis=1), 0.0, -jnp.inf)
            dq, dk, dv = terms(
                kpb[0, rows, :], kpb[1, rows, :], qpb[...].reshape(UNIT, DH), dopb[...].reshape(UNIT, DH),
                rows_p[0:1, :], rows_p[1:2, :], add,
            )
            dqpa[...] += dq
            dacc[i, 0] += dk
            dacc[i, 1] += dv

    @pl.loop(0, 8)
    def _(t):
        i = (x + 1 + t) % 4
        ch = t // 4

        @pl.when(t % 4 == 0)
        def _():
            @pl.loop(0, 2)
            def _(b):
                q1(2 * (1 - y) + b, g, ch).wait_recv()
                do1(2 * (1 - y) + b, g, ch).wait_recv()

        unit_chunk(kpb, i, 1 - y, ch)

        @pl.when(t >= 4)
        def _():
            finish(psend, prx, pps, ppr, i)

    def dqp_copy(j):
        return remote(dqp_st.at[j], dqp_out, dps.at[j], dpr.at[0], prompt=mate(j))

    own_dqp = pltpu.make_async_copy(dqp_st.at[g], dqp_out, loc.at[4])

    @pl.when(g == handler)
    def _():
        dqp_st[...] = (dqpa[...] * SCALE).astype(BF16).reshape(4, ROWS, DH)
        own_dqp.start()

        @pl.loop(1, 4)
        def _(o):
            dqp_copy((g + o) % 4).start()

    def r_copy(src, dst):
        return remote(rst.at[dst], rrcv.at[src], rss.at[dst], rsr.at[src], reply=dst)

    def final_piece(kv, i, j):
        return dkvp_out.at[kv, at(16 * i, 16, 16), group_cols(j)]

    def g_send(dst):
        piece = final_piece(r // 16, r % 4, g)
        return remote(ag_st, piece, ags.at[dst], agr.at[g, 4 * (r // 16) + r % 4], prompt=mate(turn), reply=dst)

    def g_recv(j, i):
        return remote(ag_st, final_piece(i // 4, i % 4, j), ags.at[0], agr.at[j, i], prompt=mate(j), reply=giver(i))

    own_g = pltpu.make_async_copy(ag_st, final_piece(r // 16, r % 4, g), loc.at[6])

    def others():
        for far in (2, 1, 3, 0):
            for dz in (4, 3, 5, 2, 6, 1, 7, 0):
                if far or dz:
                    yield 8 * ((r // 8 + far) % 4) + (r + dz) % 8

    def sum_column():
        totals = totals_of(psend, prx, pps, ppr)
        for kv in range(2):
            for i in range(16):
                rst[16 * kv + i] = totals[kv][16 * i:16 * i + 16]

        for other in others():
            r_copy(r, other).start()

    def sum_replies():
        total = rst[r].astype(F32)
        rrcv[r] = jnp.zeros((16, DH), BF16)

        @pl.loop(1, 32)
        def _(o):
            r_copy((r + o) % 32, r).wait_recv()

        for i in range(32):
            total = total + rrcv[i].astype(F32)
        ag_st[...] = total.astype(BF16)

        @pl.when(turn == g)
        def _():
            own_g.start()

        @pl.when(turn != g)
        def _():
            g_send(r).start()

        for other in others():
            g_send(other).start()

    dacc[...] = jnp.zeros_like(dacc)

    def dq_copy(src, dst):
        return remote(dq_st.at[dst], dqr_out.at[0, :, head_cols(src)], os_.at[dst], or_.at[src], prompt=mate(dst))

    own_dq = pltpu.make_async_copy(dq_st.at[g], dqr_out.at[0, :, head_cols(g)], loc.at[0])

    def stage_dq(half):
        part = (dqa[half] * SCALE).astype(BF16)
        for h in range(8):
            for b in range(2):
                dq_st[2 * half + b, :, DH * h:DH * h + DH] = part[HALF * h + ROWS * b:HALF * h + ROWS * b + ROWS]

    @pl.loop(0, 4)
    def _(i):
        @pl.when(i != x)
        def _():
            kr2(i, x).wait_recv()
            mk2(i, x).wait_recv()

        half = (i + 3 - x) // 4
        set_bias(i, half, HALF)
        unit(krb, i, half, HALF, True)

        @pl.when(i > x)
        def _():
            finish(rsend, rrx, rps, rpr, i)

        @pl.when(i == 2)
        def _():
            sum_column()

    stage_dq(0)

    @pl.loop(0, x + 1)
    def _(i):
        set_bias(i, 1, UNIT)
        unit(krb, i, 1, UNIT, True)
        finish(rsend, rrx, rps, rpr, i)

    stage_dq(1)
    own_dq.start()
    dq_copy(g, near).start()
    sum_replies()

    @pl.loop(0, 2)
    def _(b):
        dq_copy(g, 2 * (1 - y) + (c + b) % 2).start()

    totals = totals_of(rsend, rrx, rps, rpr)
    for kv in range(2):
        for j in range(4):
            dkv_st[j, kv] = totals[kv][ROWS * j:ROWS * j + ROWS]

    def f_copy(src, dst):
        return remote(dkv_st.at[dst], dkvr_out.at[:, 0, :, group_cols(src)], fs.at[dst], fr.at[src], prompt=mate(dst))

    own_f = pltpu.make_async_copy(dkv_st.at[g], dkvr_out.at[:, 0, :, group_cols(g)], loc.at[1])
    own_f.start()

    @pl.loop(1, 4)
    def _(o):
        f_copy(g, (g + o) % 4).start()

    own_dq.wait()
    own_f.wait()

    @pl.when(turn == g)
    def _():
        own_g.wait()

    @pl.when(turn != g)
    def _():
        g_send(r).wait_send()

    @pl.when(g == handler)
    def _():
        own_dqp.wait()

        @pl.loop(1, 4)
        def _(o):
            dqp_copy((g + o) % 4).wait_send()

    @pl.when(g != handler)
    def _():
        own_qp.wait()
        own_dop.wait()
        dqp_copy(g).wait_recv()
        for copy in hand(g):
            copy.wait_send()

    @pl.loop(1, 4)
    def _(o):
        other = (g + o) % 4
        dq_copy(other, g).wait_recv()
        kp1(g, other).wait_send()
        kr1(g, other).wait_send()
        mk1(g, other).wait_send()
        for ch in range(2):
            q1(g, other, ch).wait_send()
            do1(g, other, ch).wait_send()
        ls1(g, other).wait_send()
        dq_copy(g, other).wait_send()
        f_copy(other, g).wait_recv()
        f_copy(g, other).wait_send()
        partial(psend, prx, pps, ppr, x, (x + o) % 4).wait_send()
        partial(rsend, rrx, rps, rpr, x, (x + o) % 4).wait_send()
        ring = (x + o) % 4
        kp2(x, ring).wait_send()
        kr2(x, ring).wait_send()
        mk2(x, ring).wait_send()

    @pl.loop(0, 32)
    def _(o):
        j, i = o // 8, o % 8

        @pl.when((j != g) | (giver(i) != r))
        def _():
            g_recv(j, i).wait_recv()

    @pl.loop(1, 32)
    def _(o):
        r_copy(r, (r + o) % 32).wait_send()
        g_send((r + o) % 32).wait_send()


def call(*args):
    anywhere = pl.BlockSpec(memory_space=pl.ANY)
    vmem = pl.BlockSpec(memory_space=pltpu.VMEM)
    smem = pl.BlockSpec(memory_space=pltpu.SMEM)
    dma = pltpu.SemaphoreType.DMA
    out = jax.ShapeDtypeStruct
    four = [dma((4,))] * 2
    pairs = [dma((4, 2))] * 2
    thirtytwo = [dma((32,))] * 2
    results = pl.pallas_call(
        kernel,
        out_shape=(
            pltpu.VMEM((ROWS, DH), BF16),
            pltpu.VMEM((2, ROWS, 512), BF16),
            pltpu.VMEM((1, ROWS, 4096), BF16),
            pltpu.VMEM((2, 1, ROWS, 512), BF16),
        ),
        in_specs=[
            anywhere, anywhere, anywhere, vmem, vmem, anywhere, anywhere, anywhere, vmem, vmem, smem, vmem,
        ],
        out_specs=(vmem, vmem, vmem, vmem),
        scratch_shapes=[
            pltpu.VMEM((2, HALF, WIDE), BF16),
            pltpu.VMEM((2, HALF, WIDE), BF16),
            pltpu.VMEM((2, HALF, DH), BF16),
            pltpu.VMEM((2, HALF, DH), BF16),
            pltpu.VMEM((2, 1024, DH), BF16),
            pltpu.VMEM((2, 1024, DH), BF16),
            pltpu.VMEM((4, 2, 8, 128), F32),
            pltpu.VMEM((4, 2, 8, 128), F32),
            pltpu.VMEM((4, 8, 128), F32),
            pltpu.VMEM((4, 4, 8, 128), F32),
            pltpu.VMEM((2, 2, 1, 512), F32),
            pltpu.VMEM((2, 2, 1, 512), F32),
            pltpu.VMEM((8, UNIT), F32),
            pltpu.VMEM((UNIT, HALF), F32),
            pltpu.VMEM((2, WIDE, DH), F32),
            pltpu.VMEM((UNIT, DH), F32),
            pltpu.VMEM((4, 2, UNIT, DH), F32),
            pltpu.VMEM((2, UNIT, DH), F32),
            pltpu.VMEM((4, 2, UNIT, DH), BF16),
            pltpu.VMEM((4, 2, UNIT, DH), BF16),
            pltpu.VMEM((4, 2, UNIT, DH), BF16),
            pltpu.VMEM((4, 2, UNIT, DH), BF16),
            pltpu.VMEM((32, 16, DH), BF16),
            pltpu.VMEM((32, 16, DH), BF16),
            pltpu.VMEM((16, DH), BF16),
            pltpu.VMEM((4, ROWS, WIDE), BF16),
            pltpu.VMEM((4, ROWS, DH), BF16),
            pltpu.VMEM((4, 2, ROWS, DH), BF16),
            dma((8,)),
            *pairs,
            *pairs,
            *four,
            dma((3,)),
            dma((3, 4)),
            *four,
            *four,
            *four,
            *four,
            *four,
            *four,
            *four,
            *four,
            *thirtytwo,
            dma((32,)),
            dma((4, 8)),
            *four,
            *four,
            *four,
        ],
        compiler_params=pltpu.CompilerParams(
            collective_id=0, has_side_effects=True, vmem_limit_bytes=VMEM_LIMIT
        ),
    )(*args)

    def hand_over(*refs):
        sems = refs[-1]
        copies = [pltpu.make_async_copy(refs[i], refs[4 + i], sems.at[i]) for i in range(4)]
        for copy in copies:
            copy.start()
        for copy in copies:
            copy.wait()

    return pl.pallas_call(
        hand_over,
        out_shape=[out(a.shape, a.dtype) for a in results],
        in_specs=[anywhere] * 4,
        out_specs=[anywhere] * 4,
        scratch_shapes=[dma((4,))],
        compiler_params=pltpu.CompilerParams(vmem_limit_bytes=2**20),
    )(*results)


VMEM_LIMIT = 62 * 2**20


def solution(mesh):
    placed = (
        P("prompt", "reply"),
        P("prompt", "reply"),
        P(None, "prompt", None),
        P("reply", "prompt"),
        P("reply", "prompt"),
        P("reply", "prompt", None),
        P("reply", "prompt", None),
        P(None, "reply", "prompt", None),
        P("reply", None, "prompt"),
        P("reply", None, "prompt"),
        P("reply"),
        P("reply", "prompt"),
    )
    return jax.shard_map(
        call,
        mesh=mesh,
        in_specs=placed,
        out_specs=(
            P("prompt", "reply"),
            P(None, "prompt", None),
            P("reply", "prompt", None),
            P(None, "reply", "prompt", None),
        ),
        check_vma=False,
    )
```

```python
import jax
import jax.numpy as jnp
from jax import lax
from jax.experimental import pallas as pl
from jax.experimental.pallas import tpu as pltpu
from jax.sharding import PartitionSpec as P

MESH = pl.DeviceIdType.MESH
F32 = jnp.float32
BF16 = jnp.bfloat16
DH = 128
ROWS = 64
HALF = 128
UNIT = 256
WIDE = 1024
SCALE = DH**-0.5
LOG2E = 1.4426950408889634
NN = (((1,), (0,)), ((), ()))
NT = (((1,), (1,)), ((), ()))
TN = (((0,), (0,)), ((), ()))


def dot(a, b, dims=NN):
    return lax.dot_general(a, b, dims, preferred_element_type=F32)


def at(start, size, step):
    return pl.ds(pl.multiple_of(start, step), size)


def kernel(
    qp, dop, kvp, lsep_in, delp_in, qr, dor, kvr, lser_in, delr_in, rlen_in, rmask_in,
    dqp_out, dkvp_out, dqr_out, dkvr_out,
    lsep, delp, lser, delr, rlen, rmask, qbuf, dobuf, qpb, dopb, kpb, krb, lsd_st, lsd_rx, lsp_rx, msk, lse2, del2, rows_p, bias,
    dqa, dqpa, dacc, keep, psend, prx, rsend, rrx, rst, rrcv, ag_st, dq_st, dqp_st, dkv_st,
    loc, qs, qrx, ds, drx, ls, lrx, ps, prs, kp1s, kp1r, kr1s, kr1r, ms1, mr1, kp2s, kp2r, kr2s, kr2r, ms2, mr2,
    pps, ppr, rps, rpr, rss, rsr, ags, agr, os_, or_, fs, fr, dps, dpr,
):
    p = lax.axis_index("prompt")
    r = lax.axis_index("reply")
    y = p // 8
    x = (p // 2) % 4
    c = p % 2
    g = 2 * y + c
    yh = r // 8
    z = r % 8
    handler = r // 8
    turn = (r // 4) % 4
    beyond = 8 * ((yh + 2 * y + 3) % 4) + z
    near = 2 * y + 1 - c

    def device(i, j):
        return 8 * (j // 2) + 2 * i + j % 2

    def mate(j):
        return device(x, j)

    def along(i):
        return 8 * y + 2 * i + c

    def remote(src, dst, send, recv, **where):
        return pltpu.make_async_remote_copy(
            src_ref=src, dst_ref=dst, send_sem=send, recv_sem=recv, device_id=where, device_id_type=MESH
        )

    barrier = pltpu.get_barrier_semaphore()

    def greet(**where):
        pl.semaphore_signal(barrier, inc=1, device_id=where, device_id_type=MESH)

    @pl.loop(1, 4)
    def _(o):
        greet(prompt=mate((g + o) % 4))
        greet(prompt=along((x + o) % 4))

    @pl.loop(0, 2)
    def _(b):
        greet(prompt=mate(2 * (1 - y) + b), reply=beyond)

    @pl.loop(1, 32)
    def _(o):
        greet(reply=(r + o) % 32)

    def giver(i):
        return 16 * (i // 4) + 4 * g + i % 4

    @pl.loop(1, 4)
    def _(o):
        @pl.loop(0, 8)
        def _(i):
            greet(prompt=mate((g + o) % 4), reply=giver(i))

    small = [
        pltpu.make_async_copy(src, dst, loc.at[8 + i])
        for i, (src, dst) in enumerate(
            ((lser_in, lser), (delr_in, delr), (lsep_in, lsep), (delp_in, delp), (rlen_in, rlen), (rmask_in, rmask))
        )
    ]
    for copy in small:
        copy.start()

    def group_cols(j):
        return at(DH * j, DH, DH)

    def head_cols(j):
        return at(WIDE * j, WIDE, WIDE)

    def seat(ref, j):
        return ref.at[j // 2, at(ROWS * (j % 2), ROWS, ROWS), :]

    def rows_at(ref, i, j):
        return ref.at[:, at(UNIT * i + ROWS * j, ROWS, ROWS), :]

    def unit_at(ref, i):
        return ref.at[:, at(UNIT * i, UNIT, UNIT), :]

    own_kp = pltpu.make_async_copy(kvp.at[:, :, group_cols(g)], rows_at(kpb, x, g), loc.at[2])
    own_kr = pltpu.make_async_copy(kvr.at[:, 0, :, group_cols(g)], rows_at(krb, x, g), loc.at[3])
    own_q = pltpu.make_async_copy(qr.at[0, :, head_cols(g)], seat(qbuf, g), loc.at[0])
    own_do = pltpu.make_async_copy(dor.at[0, :, head_cols(g)], seat(dobuf, g), loc.at[1])
    own_qp = pltpu.make_async_copy(qp, seat(qpb, g), loc.at[4])
    own_dop = pltpu.make_async_copy(dop, seat(dopb, g), loc.at[5])
    for copy in (own_kp, own_q, own_do, own_kr, own_qp, own_dop):
        copy.start()

    def twice(v):
        return jnp.concatenate([v, v], axis=1)

    for copy in small:
        copy.wait()

    for j in range(4):
        lsd_st[j, 0] = twice(lser[0, 8 * j:8 * j + 8, :])
        lsd_st[j, 1] = twice(delr[0, 8 * j:8 * j + 8, :])
    lsp_rx[g, 0:1, :] = twice(lsep[...])
    lsp_rx[g, 1:2, :] = twice(delp[...])
    lsp_rx[g, 2:8, :] = jnp.zeros((6, 128), F32)
    msk[x, g] = jnp.broadcast_to(twice(rmask[...].astype(F32)), (8, 128))
    lsd_rx[g] = lsd_st[g]

    @pl.when(turn == g)
    def _():
        pl.semaphore_wait(barrier, 3 + 3 + 2 + 31)

    @pl.when(turn != g)
    def _():
        pl.semaphore_wait(barrier, 3 + 3 + 2 + 31 + 32)

    def kp1(src, dst, **where):
        piece = kvp.at[:, :, group_cols(dst)]
        return remote(piece, rows_at(kpb, x, src), kp1s.at[dst], kp1r.at[src], prompt=mate(dst), **where)

    def kr1(src, dst):
        return remote(kvr.at[:, 0, :, group_cols(dst)], rows_at(krb, x, src), kr1s.at[dst], kr1r.at[src], prompt=mate(dst))

    def mk1(src, dst):
        return remote(msk.at[x, src], msk.at[x, src], ms1.at[dst], mr1.at[src], prompt=mate(dst))

    def chunk(ref, j, ch):
        return ref.at[j // 2, at(ROWS * (j % 2), ROWS, ROWS), at(512 * ch, 512, 512)]

    def q1(src, dst, ch):
        piece = qr.at[0, :, at(WIDE * dst + 512 * ch, 512, 512)]
        return remote(piece, chunk(qbuf, src, ch), qs.at[dst, ch], qrx.at[src, ch], prompt=mate(dst))

    def do1(src, dst, ch):
        piece = dor.at[0, :, at(WIDE * dst + 512 * ch, 512, 512)]
        return remote(piece, chunk(dobuf, src, ch), ds.at[dst, ch], drx.at[src, ch], prompt=mate(dst))

    def ls1(src, dst):
        return remote(lsd_st.at[dst], lsd_rx.at[src], ls.at[dst], lrx.at[src], prompt=mate(dst))

    def hand(src):
        return [
            remote(qp, seat(qpb, src), ps.at[0], prs.at[0, src], prompt=mate(handler)),
            remote(dop, seat(dopb, src), ps.at[1], prs.at[1, src], prompt=mate(handler)),
            remote(lsp_rx.at[src], lsp_rx.at[src], ps.at[2], prs.at[2, src], prompt=mate(handler)),
        ]

    @pl.loop(0, 2)
    def _(b):
        kp1(g, 2 * (1 - y) + (c + b) % 2, reply=beyond).start()

    kp1(g, near).start()

    ls1(g, near).start()
    for ch in range(2):
        q1(g, near, ch).start()
        do1(g, near, ch).start()

    @pl.loop(0, 2)
    def _(b):
        far = 2 * (1 - y) + (c + b) % 2
        ls1(g, far).start()
        kr1(g, far).start()
        mk1(g, far).start()

    kr1(g, near).start()
    mk1(g, near).start()

    @pl.when(g != handler)
    def _():
        for copy in hand(g):
            copy.start()

    @pl.loop(0, 4)
    def _(b):
        far = 2 * (1 - y) + (c + b) % 2
        q1(g, far, b // 2).start()
        do1(g, far, b // 2).start()

    def kp2(src, dst):
        return remote(unit_at(kpb, src), unit_at(kpb, src), kp2s.at[dst], kp2r.at[src], prompt=along(dst))

    def kr2(src, dst):
        return remote(unit_at(krb, src), unit_at(krb, src), kr2s.at[dst], kr2r.at[src], prompt=along(dst))

    def mk2(src, dst):
        return remote(msk.at[src], msk.at[src], ms2.at[dst], mr2.at[src], prompt=along(dst))

    own_kp.wait()

    @pl.loop(1, 4)
    def _(o):
        kp1((g + o) % 4, g).wait_recv()

    @pl.loop(1, 4)
    def _(o):
        kp2(x, (x + 4 - o) % 4).start()

    dqa[...] = jnp.zeros_like(dqa)
    dacc[...] = jnp.zeros_like(dacc)

    def pass_reply_keys():
        own_kr.wait()

        @pl.loop(1, 4)
        def _(o):
            kr1((g + o) % 4, g).wait_recv()
            mk1((g + o) % 4, g).wait_recv()

        @pl.loop(1, 4)
        def _(o):
            kr2(x, (x + 4 - o) % 4).start()
            mk2(x, (x + 4 - o) % 4).start()

    pass_reply_keys()

    lane = lax.broadcasted_iota(jnp.int32, (1, 128), 1)
    first = lane < 64

    def rows_of(half):
        alive = HALF * x + 512 * half + lane < rlen[0]
        lse = jnp.where(first, lsd_rx[2 * half, 0], lsd_rx[2 * half + 1, 0]) * LOG2E
        lse = jnp.where(alive, lse, jnp.inf)
        delta = jnp.where(first, lsd_rx[2 * half, 1], lsd_rx[2 * half + 1, 1])
        for ch in range(2):
            lse2[half, ch] = jnp.concatenate([lse[h:h + 1] for h in range(4 * ch, 4 * ch + 4)], axis=1)
            del2[half, ch] = jnp.concatenate([delta[h:h + 1] for h in range(4 * ch, 4 * ch + 4)], axis=1)

    own_q.wait()
    own_do.wait()
    for ch in range(2):
        q1(near, g, ch).wait_recv()
        do1(near, g, ch).wait_recv()
    ls1(near, g).wait_recv()
    rows_of(y)

    def heads(ref, half):
        return jnp.concatenate([ref[half, :, DH * h:DH * h + DH] for h in range(8)], axis=0)

    def terms(keys, vals, q, do, lse_row, del_row, add):
        score = dot(keys, q, NT) * (SCALE * LOG2E) - lse_row
        if add is not None:
            score = score + add
        prob = jnp.exp2(score)
        dprob = dot(vals, do, NT)
        prob_b = prob.astype(BF16)
        ds_b = (prob * (dprob - del_row)).astype(BF16)
        return dot(ds_b, keys, TN), dot(ds_b, q), dot(prob_b, do)

    def both(ref, half):
        return jnp.concatenate([ref[half, 0], ref[half, 1]], axis=1)

    def unit(ref, i, half, size, masked):
        rows = at(UNIT * i, size, UNIT)
        add = None
        if masked:
            add = jnp.concatenate([bias[0:size, :]] * 8, axis=1)
        dq, dk, dv = terms(
            ref[0, rows, :], ref[1, rows, :], heads(qbuf, half), heads(dobuf, half), both(lse2, half), both(del2, half), add
        )
        dqa[half] += dq
        dacc[i, 0, 0:size, :] += dk
        dacc[i, 1, 0:size, :] += dv

    def four(ref, half, ch):
        return jnp.concatenate([ref[half, :, at(512 * ch + DH * h, DH, DH)] for h in range(4)], axis=0)

    def unit_chunk(ref, i, half, ch):
        rows = at(UNIT * i, UNIT, UNIT)
        dq, dk, dv = terms(
            ref[0, rows, :], ref[1, rows, :], four(qbuf, half, ch), four(dobuf, half, ch), lse2[half, ch], del2[half, ch], None
        )
        dqa[half, at(512 * ch, 512, 512), :] += dq
        dacc[i, 0] += dk
        dacc[i, 1] += dv

    def causal(i, half, size):
        key = lax.broadcasted_iota(jnp.int32, (HALF, HALF), 0)
        query = lax.broadcasted_iota(jnp.int32, (HALF, HALF), 1)
        return [key - query <= HALF * x + 512 * half - HALF * i - 512 * b for b in range(size // HALF)]

    def set_bias(i, half, size):
        for b, ok in enumerate(causal(i, half, size)):
            row = jnp.where(first, msk[i, 2 * b, 0:1, :], msk[i, 2 * b + 1, 0:1, :])
            column = jnp.transpose(jnp.broadcast_to(row, (HALF, HALF)))
            bias[HALF * b:HALF * b + HALF, :] = jnp.where(ok & (column > 0.5), 0.0, -jnp.inf)

    def partial(buf, rx, send, recv, src, dst):
        return remote(buf.at[dst], rx.at[src], send.at[dst], recv.at[src], prompt=along(dst))

    def finish(buf, rx, send, recv, i):
        @pl.when(i == x)
        def _():
            keep[0] = dacc[x, 0] * SCALE
            keep[1] = dacc[x, 1]

        @pl.when(i != x)
        def _():
            buf[i, 0] = (dacc[i, 0] * SCALE).astype(BF16)
            buf[i, 1] = dacc[i, 1].astype(BF16)
            partial(buf, rx, send, recv, x, i).start()

    def totals_of(buf, rx, send, recv):
        @pl.loop(1, 4)
        def _(o):
            partial(buf, rx, send, recv, (x + o) % 4, x).wait_recv()

        totals = []
        for kv in range(2):
            total = keep[kv]
            for o in range(1, 4):
                total = total + rx[(x + o) % 4, kv].astype(F32)
            totals.append(total.astype(BF16))
        return totals

    @pl.loop(0, 4)
    def _(t):
        i = (x + t) % 4

        @pl.when(t > 0)
        def _():
            kp2(i, x).wait_recv()

        unit(kpb, i, y, UNIT, False)

    @pl.loop(0, 2)
    def _(b):
        ls1(2 * (1 - y) + b, g).wait_recv()

    rows_of(1 - y)

    @pl.when(g == handler)
    def _():
        own_qp.wait()
        own_dop.wait()

        @pl.loop(1, 4)
        def _(o):
            for copy in hand((g + o) % 4):
                copy.wait_recv()

        for b in range(2):
            lse = jnp.where(first, lsp_rx[2 * b, 0:1, :], lsp_rx[2 * b + 1, 0:1, :]) * LOG2E
            delta = jnp.where(first, lsp_rx[2 * b, 1:2, :], lsp_rx[2 * b + 1, 1:2, :])
            rows_p[0:1, DH * b:DH * b + DH] = lse
            rows_p[1:2, DH * b:DH * b + DH] = delta
        dqpa[...] = jnp.zeros_like(dqpa)

        @pl.loop(0, 4)
        def _(i):
            rows = at(UNIT * i, UNIT, UNIT)
            grid = [jnp.concatenate(causal(i, b, UNIT), axis=0) for b in range(2)]
            add = jnp.where(jnp.concatenate(grid, axis=1), 0.0, -jnp.inf)
            dq, dk, dv = terms(
                kpb[0, rows, :], kpb[1, rows, :], qpb[...].reshape(UNIT, DH), dopb[...].reshape(UNIT, DH),
                rows_p[0:1, :], rows_p[1:2, :], add,
            )
            dqpa[...] += dq
            dacc[i, 0] += dk
            dacc[i, 1] += dv

    @pl.loop(0, 8)
    def _(t):
        i = (x + 1 + t) % 4
        ch = t // 4

        @pl.when(t % 4 == 0)
        def _():
            @pl.loop(0, 2)
            def _(b):
                q1(2 * (1 - y) + b, g, ch).wait_recv()
                do1(2 * (1 - y) + b, g, ch).wait_recv()

        unit_chunk(kpb, i, 1 - y, ch)

        @pl.when(t >= 4)
        def _():
            finish(psend, prx, pps, ppr, i)

    def dqp_copy(j):
        return remote(dqp_st.at[j], dqp_out, dps.at[j], dpr.at[0], prompt=mate(j))

    own_dqp = pltpu.make_async_copy(dqp_st.at[g], dqp_out, loc.at[4])

    @pl.when(g == handler)
    def _():
        dqp_st[...] = (dqpa[...] * SCALE).astype(BF16).reshape(4, ROWS, DH)
        own_dqp.start()

        @pl.loop(1, 4)
        def _(o):
            dqp_copy((g + o) % 4).start()

    def r_copy(src, dst):
        return remote(rst.at[dst], rrcv.at[src], rss.at[dst], rsr.at[src], reply=dst)

    def final_piece(kv, i, j):
        return dkvp_out.at[kv, at(16 * i, 16, 16), group_cols(j)]

    def g_send(dst):
        piece = final_piece(r // 16, r % 4, g)
        return remote(ag_st, piece, ags.at[dst], agr.at[g, 4 * (r // 16) + r % 4], prompt=mate(turn), reply=dst)

    def g_recv(j, i):
        return remote(ag_st, final_piece(i // 4, i % 4, j), ags.at[0], agr.at[j, i], prompt=mate(j), reply=giver(i))

    own_g = pltpu.make_async_copy(ag_st, final_piece(r // 16, r % 4, g), loc.at[6])

    def others():
        for far in (2, 1, 3, 0):
            for dz in (4, 3, 5, 2, 6, 1, 7, 0):
                if far or dz:
                    yield 8 * ((r // 8 + far) % 4) + (r + dz) % 8

    def sum_column():
        totals = totals_of(psend, prx, pps, ppr)
        for kv in range(2):
            for i in range(16):
                rst[16 * kv + i] = totals[kv][16 * i:16 * i + 16]

        for other in others():
            r_copy(r, other).start()

    def sum_replies():
        total = rst[r].astype(F32)
        rrcv[r] = jnp.zeros((16, DH), BF16)

        @pl.loop(1, 32)
        def _(o):
            r_copy((r + o) % 32, r).wait_recv()

        for i in range(32):
            total = total + rrcv[i].astype(F32)
        ag_st[...] = total.astype(BF16)

        @pl.when(turn == g)
        def _():
            own_g.start()

        @pl.when(turn != g)
        def _():
            g_send(r).start()

        for other in others():
            g_send(other).start()

    dacc[...] = jnp.zeros_like(dacc)

    def dq_copy(src, dst):
        return remote(dq_st.at[dst], dqr_out.at[0, :, head_cols(src)], os_.at[dst], or_.at[src], prompt=mate(dst))

    own_dq = pltpu.make_async_copy(dq_st.at[g], dqr_out.at[0, :, head_cols(g)], loc.at[0])

    def stage_dq(half):
        part = (dqa[half] * SCALE).astype(BF16)
        for h in range(8):
            for b in range(2):
                dq_st[2 * half + b, :, DH * h:DH * h + DH] = part[HALF * h + ROWS * b:HALF * h + ROWS * b + ROWS]

    def send_near():
        stage_dq(y)
        own_dq.start()
        dq_copy(g, near).start()

    def send_far():
        stage_dq(1 - y)

        @pl.loop(0, 2)
        def _(b):
            dq_copy(g, 2 * (1 - y) + (c + b) % 2).start()

    ahead = (y == 1) | (x == 3)

    @pl.loop(0, 2)
    def _(stage):
        @pl.when((stage + y) % 2 == 1)
        def _():
            @pl.loop(0, 4)
            def _(i):
                @pl.when((stage == 0) & (i != x))
                def _():
                    kr2(i, x).wait_recv()
                    mk2(i, x).wait_recv()

                @pl.when((stage == 1) & (i > x))
                def _():
                    kr2(i, x).wait_recv()
                    mk2(i, x).wait_recv()

                half = (i + 3 - x) // 4
                set_bias(i, half, HALF)
                unit(krb, i, half, HALF, True)

                @pl.when((i > x) | (stage == 1))
                def _():
                    finish(rsend, rrx, rps, rpr, i)

                @pl.when((stage == 0) & (i == 2))
                def _():
                    sum_column()

        @pl.when((stage + y) % 2 == 0)
        def _():
            @pl.loop(0, x + 1)
            def _(i):
                @pl.when((stage == 0) & (i != x))
                def _():
                    kr2(i, x).wait_recv()
                    mk2(i, x).wait_recv()

                set_bias(i, 1, UNIT)
                unit(krb, i, 1, UNIT, True)

                @pl.when(stage == 1)
                def _():
                    finish(rsend, rrx, rps, rpr, i)

                @pl.when((stage == 0) & (i == (x + 2) // 3))
                def _():
                    sum_column()

        @pl.when((stage == 0) & ahead)
        def _():
            send_far()

    @pl.when((y == 0) & (x != 3))
    def _():
        send_far()

    sum_replies()
    send_near()

    totals = totals_of(rsend, rrx, rps, rpr)
    for kv in range(2):
        for j in range(4):
            dkv_st[j, kv] = totals[kv][ROWS * j:ROWS * j + ROWS]

    def f_copy(src, dst):
        return remote(dkv_st.at[dst], dkvr_out.at[:, 0, :, group_cols(src)], fs.at[dst], fr.at[src], prompt=mate(dst))

    own_f = pltpu.make_async_copy(dkv_st.at[g], dkvr_out.at[:, 0, :, group_cols(g)], loc.at[1])
    own_f.start()

    @pl.loop(1, 4)
    def _(o):
        f_copy(g, (g + o) % 4).start()

    @pl.when(g == handler)
    def _():
        own_dqp.wait()

        @pl.loop(1, 4)
        def _(o):
            dqp_copy((g + o) % 4).wait_send()

    @pl.when(g != handler)
    def _():
        own_qp.wait()
        own_dop.wait()
        for copy in hand(g):
            copy.wait_send()

    @pl.loop(1, 4)
    def _(o):
        other = (g + o) % 4
        kp1(g, other).wait_send()
        kr1(g, other).wait_send()
        mk1(g, other).wait_send()
        for ch in range(2):
            q1(g, other, ch).wait_send()
            do1(g, other, ch).wait_send()
        ls1(g, other).wait_send()
        ring = (x + o) % 4
        kp2(x, ring).wait_send()
        kr2(x, ring).wait_send()
        mk2(x, ring).wait_send()
        partial(psend, prx, pps, ppr, x, ring).wait_send()
        partial(rsend, rrx, rps, rpr, x, ring).wait_send()

    @pl.loop(1, 32)
    def _(o):
        r_copy(r, (r + o) % 32).wait_send()

    @pl.when(turn == g)
    def _():
        own_g.wait()

    @pl.when(turn != g)
    def _():
        g_send(r).wait_send()

    @pl.loop(1, 32)
    def _(o):
        g_send((r + o) % 32).wait_send()

    @pl.loop(1, 4)
    def _(o):
        dq_copy(g, (g + o) % 4).wait_send()
        f_copy(g, (g + o) % 4).wait_send()

    own_dq.wait()
    own_f.wait()

    @pl.when(g != handler)
    def _():
        dqp_copy(g).wait_recv()

    @pl.loop(1, 4)
    def _(o):
        dq_copy((g + o) % 4, g).wait_recv()
        f_copy((g + o) % 4, g).wait_recv()

    @pl.loop(0, 32)
    def _(o):
        j, i = o // 8, o % 8

        @pl.when((j != g) | (giver(i) != r))
        def _():
            g_recv(j, i).wait_recv()


def call(*args):
    anywhere = pl.BlockSpec(memory_space=pl.ANY)
    vmem = pl.BlockSpec(memory_space=pltpu.VMEM)
    dma = pltpu.SemaphoreType.DMA
    out = jax.ShapeDtypeStruct
    four = [dma((4,))] * 2
    pairs = [dma((4, 2))] * 2
    thirtytwo = [dma((32,))] * 2
    results = pl.pallas_call(
        kernel,
        out_shape=(
            pltpu.VMEM((ROWS, DH), BF16),
            pltpu.VMEM((2, ROWS, 512), BF16),
            pltpu.VMEM((1, ROWS, 4096), BF16),
            pltpu.VMEM((2, 1, ROWS, 512), BF16),
        ),
        in_specs=[
            anywhere,
        ] * 12,
        out_specs=(vmem, vmem, vmem, vmem),
        scratch_shapes=[
            pltpu.VMEM((1, ROWS), F32),
            pltpu.VMEM((1, ROWS), F32),
            pltpu.VMEM((1, 32, ROWS), F32),
            pltpu.VMEM((1, 32, ROWS), F32),
            pltpu.SMEM((1,), jnp.int32),
            pltpu.VMEM((1, ROWS), jnp.int32),
            pltpu.VMEM((2, HALF, WIDE), BF16),
            pltpu.VMEM((2, HALF, WIDE), BF16),
            pltpu.VMEM((2, HALF, DH), BF16),
            pltpu.VMEM((2, HALF, DH), BF16),
            pltpu.VMEM((2, 1024, DH), BF16),
            pltpu.VMEM((2, 1024, DH), BF16),
            pltpu.VMEM((4, 2, 8, 128), F32),
            pltpu.VMEM((4, 2, 8, 128), F32),
            pltpu.VMEM((4, 8, 128), F32),
            pltpu.VMEM((4, 4, 8, 128), F32),
            pltpu.VMEM((2, 2, 1, 512), F32),
            pltpu.VMEM((2, 2, 1, 512), F32),
            pltpu.VMEM((8, UNIT), F32),
            pltpu.VMEM((UNIT, HALF), F32),
            pltpu.VMEM((2, WIDE, DH), F32),
            pltpu.VMEM((UNIT, DH), F32),
            pltpu.VMEM((4, 2, UNIT, DH), F32),
            pltpu.VMEM((2, UNIT, DH), F32),
            pltpu.VMEM((4, 2, UNIT, DH), BF16),
            pltpu.VMEM((4, 2, UNIT, DH), BF16),
            pltpu.VMEM((4, 2, UNIT, DH), BF16),
            pltpu.VMEM((4, 2, UNIT, DH), BF16),
            pltpu.VMEM((32, 16, DH), BF16),
            pltpu.VMEM((32, 16, DH), BF16),
            pltpu.VMEM((16, DH), BF16),
            pltpu.VMEM((4, ROWS, WIDE), BF16),
            pltpu.VMEM((4, ROWS, DH), BF16),
            pltpu.VMEM((4, 2, ROWS, DH), BF16),
            dma((14,)),
            *pairs,
            *pairs,
            *four,
            dma((3,)),
            dma((3, 4)),
            *four,
            *four,
            *four,
            *four,
            *four,
            *four,
            *four,
            *four,
            *thirtytwo,
            dma((32,)),
            dma((4, 8)),
            *four,
            *four,
            *four,
        ],
        compiler_params=pltpu.CompilerParams(
            collective_id=0, has_side_effects=True, vmem_limit_bytes=VMEM_LIMIT
        ),
    )(*args)

    def hand_over(*refs):
        sems = refs[-1]
        copies = [pltpu.make_async_copy(refs[i], refs[4 + i], sems.at[i]) for i in range(4)]
        for copy in copies:
            copy.start()
        for copy in copies:
            copy.wait()

    return pl.pallas_call(
        hand_over,
        out_shape=[out(a.shape, a.dtype) for a in results],
        in_specs=[anywhere] * 4,
        out_specs=[anywhere] * 4,
        scratch_shapes=[dma((4,))],
        compiler_params=pltpu.CompilerParams(vmem_limit_bytes=2**20),
    )(*results)


VMEM_LIMIT = 62 * 2**20


def solution(mesh):
    placed = (
        P("prompt", "reply"),
        P("prompt", "reply"),
        P(None, "prompt", None),
        P("reply", "prompt"),
        P("reply", "prompt"),
        P("reply", "prompt", None),
        P("reply", "prompt", None),
        P(None, "reply", "prompt", None),
        P("reply", None, "prompt"),
        P("reply", None, "prompt"),
        P("reply"),
        P("reply", "prompt"),
    )
    return jax.shard_map(
        call,
        mesh=mesh,
        in_specs=placed,
        out_specs=(
            P("prompt", "reply"),
            P(None, "prompt", None),
            P("reply", "prompt", None),
            P(None, "reply", "prompt", None),
        ),
        check_vma=False,
    )
```

```python
import jax
import jax.numpy as jnp
from jax import lax
from jax.experimental import pallas as pl
from jax.experimental.pallas import tpu as pltpu
from jax.sharding import PartitionSpec as P

MESH = pl.DeviceIdType.MESH
F32 = jnp.float32
BF16 = jnp.bfloat16
DH = 128
ROWS = 64
HALF = 128
UNIT = 256
WIDE = 1024
SCALE = DH**-0.5
LOG2E = 1.4426950408889634
NN = (((1,), (0,)), ((), ()))
NT = (((1,), (1,)), ((), ()))
TN = (((0,), (0,)), ((), ()))


def dot(a, b, dims=NN):
    return lax.dot_general(a, b, dims, preferred_element_type=F32)


def at(start, size, step):
    return pl.ds(pl.multiple_of(start, step), size)


def kernel(
    qp, dop, kvp, lsep_in, delp_in, qr, dor, kvr, lser_in, delr_in, rlen_in, rmask_in,
    dqp_out, dkvp_out, dqr_out, dkvr_out,
    lsep, delp, lser, delr, rlen, rmask, qbuf, dobuf, qpb, dopb, kpb, krb, lsd_st, lsd_rx, lsp_rx, msk, lse2, del2, rows_p, bias,
    dqa, dqpa, dacc, keep, psend, prx, rsend, rrx, rst, rrcv, ag_st, dq_st, dqp_st, dkv_st,
    loc, qs, qrx, ds, drx, ls, lrx, ps, prs, kp1s, kp1r, kr1s, kr1r, ms1, mr1, kp2s, kp2r, kr2s, kr2r, ms2, mr2,
    pps, ppr, rps, rpr, rss, rsr, ags, agr, os_, or_, fs, fr, dps, dpr,
):
    p = lax.axis_index("prompt")
    r = lax.axis_index("reply")
    y = p // 8
    x = (p // 2) % 4
    c = p % 2
    g = 2 * y + c
    yh = r // 8
    z = r % 8
    handler = r // 8
    turn = (r // 4) % 4
    beyond = 8 * ((yh + 2 * y + 3) % 4) + z
    near = 2 * y + 1 - c

    def device(i, j):
        return 8 * (j // 2) + 2 * i + j % 2

    def mate(j):
        return device(x, j)

    def along(i):
        return 8 * y + 2 * i + c

    def remote(src, dst, send, recv, **where):
        return pltpu.make_async_remote_copy(
            src_ref=src, dst_ref=dst, send_sem=send, recv_sem=recv, device_id=where, device_id_type=MESH
        )

    barrier = pltpu.get_barrier_semaphore()

    def greet(**where):
        pl.semaphore_signal(barrier, inc=1, device_id=where, device_id_type=MESH)

    @pl.loop(1, 4)
    def _(o):
        greet(prompt=mate((g + o) % 4))
        greet(prompt=along((x + o) % 4))

    @pl.loop(0, 2)
    def _(b):
        greet(prompt=mate(2 * (1 - y) + b), reply=beyond)

    @pl.loop(1, 32)
    def _(o):
        greet(reply=(r + o) % 32)

    def giver(i):
        return 16 * (i // 4) + 4 * g + i % 4

    @pl.loop(1, 4)
    def _(o):
        @pl.loop(0, 8)
        def _(i):
            greet(prompt=mate((g + o) % 4), reply=giver(i))

    small = [
        pltpu.make_async_copy(src, dst, loc.at[8 + i])
        for i, (src, dst) in enumerate(
            ((lser_in, lser), (delr_in, delr), (lsep_in, lsep), (delp_in, delp), (rlen_in, rlen), (rmask_in, rmask))
        )
    ]
    for copy in small:
        copy.start()

    def group_cols(j):
        return at(DH * j, DH, DH)

    def head_cols(j):
        return at(WIDE * j, WIDE, WIDE)

    def seat(ref, j):
        return ref.at[j // 2, at(ROWS * (j % 2), ROWS, ROWS), :]

    def rows_at(ref, i, j):
        return ref.at[:, at(UNIT * i + ROWS * j, ROWS, ROWS), :]

    def unit_at(ref, i):
        return ref.at[:, at(UNIT * i, UNIT, UNIT), :]

    own_kp = pltpu.make_async_copy(kvp.at[:, :, group_cols(g)], rows_at(kpb, x, g), loc.at[2])
    own_kr = pltpu.make_async_copy(kvr.at[:, 0, :, group_cols(g)], rows_at(krb, x, g), loc.at[3])
    own_q = pltpu.make_async_copy(qr.at[0, :, head_cols(g)], seat(qbuf, g), loc.at[0])
    own_do = pltpu.make_async_copy(dor.at[0, :, head_cols(g)], seat(dobuf, g), loc.at[1])
    own_qp = pltpu.make_async_copy(qp, seat(qpb, g), loc.at[4])
    own_dop = pltpu.make_async_copy(dop, seat(dopb, g), loc.at[5])
    for copy in (own_kp, own_q, own_do, own_kr, own_qp, own_dop):
        copy.start()

    def twice(v):
        return jnp.concatenate([v, v], axis=1)

    for copy in small:
        copy.wait()

    for j in range(4):
        lsd_st[j, 0] = twice(lser[0, 8 * j:8 * j + 8, :])
        lsd_st[j, 1] = twice(delr[0, 8 * j:8 * j + 8, :])
    lsp_rx[g, 0:1, :] = twice(lsep[...])
    lsp_rx[g, 1:2, :] = twice(delp[...])
    lsp_rx[g, 2:8, :] = jnp.zeros((6, 128), F32)
    msk[x, g] = jnp.broadcast_to(twice(rmask[...].astype(F32)), (8, 128))
    lsd_rx[g] = lsd_st[g]

    @pl.when(turn == g)
    def _():
        pl.semaphore_wait(barrier, 3 + 3 + 2 + 31)

    @pl.when(turn != g)
    def _():
        pl.semaphore_wait(barrier, 3 + 3 + 2 + 31 + 32)

    def kp1(src, dst, **where):
        piece = kvp.at[:, :, group_cols(dst)]
        return remote(piece, rows_at(kpb, x, src), kp1s.at[dst], kp1r.at[src], prompt=mate(dst), **where)

    def kr1(src, dst):
        return remote(kvr.at[:, 0, :, group_cols(dst)], rows_at(krb, x, src), kr1s.at[dst], kr1r.at[src], prompt=mate(dst))

    def mk1(src, dst):
        return remote(msk.at[x, src], msk.at[x, src], ms1.at[dst], mr1.at[src], prompt=mate(dst))

    def chunk(ref, j, ch):
        return ref.at[j // 2, at(ROWS * (j % 2), ROWS, ROWS), at(512 * ch, 512, 512)]

    def q1(src, dst, ch):
        piece = qr.at[0, :, at(WIDE * dst + 512 * ch, 512, 512)]
        return remote(piece, chunk(qbuf, src, ch), qs.at[dst, ch], qrx.at[src, ch], prompt=mate(dst))

    def do1(src, dst, ch):
        piece = dor.at[0, :, at(WIDE * dst + 512 * ch, 512, 512)]
        return remote(piece, chunk(dobuf, src, ch), ds.at[dst, ch], drx.at[src, ch], prompt=mate(dst))

    def ls1(src, dst):
        return remote(lsd_st.at[dst], lsd_rx.at[src], ls.at[dst], lrx.at[src], prompt=mate(dst))

    def hand(src):
        return [
            remote(qp, seat(qpb, src), ps.at[0], prs.at[0, src], prompt=mate(handler)),
            remote(dop, seat(dopb, src), ps.at[1], prs.at[1, src], prompt=mate(handler)),
            remote(lsp_rx.at[src], lsp_rx.at[src], ps.at[2], prs.at[2, src], prompt=mate(handler)),
        ]

    @pl.loop(0, 2)
    def _(b):
        kp1(g, 2 * (1 - y) + (c + b) % 2, reply=beyond).start()

    kp1(g, near).start()

    ls1(g, near).start()
    for ch in range(2):
        q1(g, near, ch).start()
        do1(g, near, ch).start()

    @pl.loop(0, 2)
    def _(b):
        far = 2 * (1 - y) + (c + b) % 2
        ls1(g, far).start()
        kr1(g, far).start()
        mk1(g, far).start()

    kr1(g, near).start()
    mk1(g, near).start()

    @pl.when(g != handler)
    def _():
        for copy in hand(g):
            copy.start()

    @pl.loop(0, 4)
    def _(b):
        far = 2 * (1 - y) + (c + b) % 2
        q1(g, far, b // 2).start()
        do1(g, far, b // 2).start()

    def kp2(src, dst):
        return remote(unit_at(kpb, src), unit_at(kpb, src), kp2s.at[dst], kp2r.at[src], prompt=along(dst))

    def kr2(src, dst):
        return remote(unit_at(krb, src), unit_at(krb, src), kr2s.at[dst], kr2r.at[src], prompt=along(dst))

    def mk2(src, dst):
        return remote(msk.at[src], msk.at[src], ms2.at[dst], mr2.at[src], prompt=along(dst))

    own_kp.wait()

    @pl.loop(1, 4)
    def _(o):
        kp1((g + o) % 4, g).wait_recv()

    @pl.loop(1, 4)
    def _(o):
        kp2(x, (x + 4 - o) % 4).start()

    dqa[...] = jnp.zeros_like(dqa)
    dacc[...] = jnp.zeros_like(dacc)

    def pass_reply_keys():
        own_kr.wait()

        @pl.loop(1, 4)
        def _(o):
            kr1((g + o) % 4, g).wait_recv()
            mk1((g + o) % 4, g).wait_recv()

        @pl.loop(1, 4)
        def _(o):
            kr2(x, (x + 4 - o) % 4).start()
            mk2(x, (x + 4 - o) % 4).start()

    pass_reply_keys()

    lane = lax.broadcasted_iota(jnp.int32, (1, 128), 1)
    first = lane < 64

    def rows_of(half):
        alive = HALF * x + 512 * half + lane < rlen[0]
        lse = jnp.where(first, lsd_rx[2 * half, 0], lsd_rx[2 * half + 1, 0]) * LOG2E
        lse = jnp.where(alive, lse, jnp.inf)
        delta = jnp.where(first, lsd_rx[2 * half, 1], lsd_rx[2 * half + 1, 1])
        for ch in range(2):
            lse2[half, ch] = jnp.concatenate([lse[h:h + 1] for h in range(4 * ch, 4 * ch + 4)], axis=1)
            del2[half, ch] = jnp.concatenate([delta[h:h + 1] for h in range(4 * ch, 4 * ch + 4)], axis=1)

    own_q.wait()
    own_do.wait()
    for ch in range(2):
        q1(near, g, ch).wait_recv()
        do1(near, g, ch).wait_recv()
    ls1(near, g).wait_recv()
    rows_of(y)

    def heads(ref, half):
        return jnp.concatenate([ref[half, :, DH * h:DH * h + DH] for h in range(8)], axis=0)

    def terms(keys, vals, q, do, lse_row, del_row, add):
        score = dot(keys, q, NT) * (SCALE * LOG2E) - lse_row
        if add is not None:
            score = score + add
        prob = jnp.exp2(score)
        dprob = dot(vals, do, NT)
        prob_b = prob.astype(BF16)
        ds_b = (prob * (dprob - del_row)).astype(BF16)
        return dot(ds_b, keys, TN), dot(ds_b, q), dot(prob_b, do)

    def both(ref, half):
        return jnp.concatenate([ref[half, 0], ref[half, 1]], axis=1)

    def unit(ref, i, half, size, masked):
        rows = at(UNIT * i, size, UNIT)
        add = None
        if masked:
            add = jnp.concatenate([bias[0:size, :]] * 8, axis=1)
        dq, dk, dv = terms(
            ref[0, rows, :], ref[1, rows, :], heads(qbuf, half), heads(dobuf, half), both(lse2, half), both(del2, half), add
        )
        dqa[half] += dq
        dacc[i, 0, 0:size, :] += dk
        dacc[i, 1, 0:size, :] += dv

    def four(ref, half, ch):
        return jnp.concatenate([ref[half, :, at(512 * ch + DH * h, DH, DH)] for h in range(4)], axis=0)

    def unit_chunk(ref, i, half, ch):
        rows = at(UNIT * i, UNIT, UNIT)
        dq, dk, dv = terms(
            ref[0, rows, :], ref[1, rows, :], four(qbuf, half, ch), four(dobuf, half, ch), lse2[half, ch], del2[half, ch], None
        )
        dqa[half, at(512 * ch, 512, 512), :] += dq
        dacc[i, 0] += dk
        dacc[i, 1] += dv

    def causal(i, half, size):
        key = lax.broadcasted_iota(jnp.int32, (HALF, HALF), 0)
        query = lax.broadcasted_iota(jnp.int32, (HALF, HALF), 1)
        return [key - query <= HALF * x + 512 * half - HALF * i - 512 * b for b in range(size // HALF)]

    def set_bias(i, half, size):
        for b, ok in enumerate(causal(i, half, size)):
            row = jnp.where(first, msk[i, 2 * b, 0:1, :], msk[i, 2 * b + 1, 0:1, :])
            column = jnp.transpose(jnp.broadcast_to(row, (HALF, HALF)))
            bias[HALF * b:HALF * b + HALF, :] = jnp.where(ok & (column > 0.5), 0.0, -jnp.inf)

    def partial(buf, rx, send, recv, src, dst):
        return remote(buf.at[dst], rx.at[src], send.at[dst], recv.at[src], prompt=along(dst))

    def finish(buf, rx, send, recv, i):
        @pl.when(i == x)
        def _():
            keep[0] = dacc[x, 0] * SCALE
            keep[1] = dacc[x, 1]

        @pl.when(i != x)
        def _():
            buf[i, 0] = (dacc[i, 0] * SCALE).astype(BF16)
            buf[i, 1] = dacc[i, 1].astype(BF16)
            partial(buf, rx, send, recv, x, i).start()

    def totals_of(buf, rx, send, recv):
        @pl.loop(1, 4)
        def _(o):
            partial(buf, rx, send, recv, (x + o) % 4, x).wait_recv()

        totals = []
        for kv in range(2):
            total = keep[kv]
            for o in range(1, 4):
                total = total + rx[(x + o) % 4, kv].astype(F32)
            totals.append(total.astype(BF16))
        return totals

    @pl.loop(0, 4)
    def _(t):
        i = (x + t) % 4

        @pl.when(t > 0)
        def _():
            kp2(i, x).wait_recv()

        unit(kpb, i, y, UNIT, False)

    @pl.loop(0, 2)
    def _(b):
        ls1(2 * (1 - y) + b, g).wait_recv()

    rows_of(1 - y)

    @pl.when(g == handler)
    def _():
        own_qp.wait()
        own_dop.wait()

        @pl.loop(1, 4)
        def _(o):
            for copy in hand((g + o) % 4):
                copy.wait_recv()

        for b in range(2):
            lse = jnp.where(first, lsp_rx[2 * b, 0:1, :], lsp_rx[2 * b + 1, 0:1, :]) * LOG2E
            delta = jnp.where(first, lsp_rx[2 * b, 1:2, :], lsp_rx[2 * b + 1, 1:2, :])
            rows_p[0:1, DH * b:DH * b + DH] = lse
            rows_p[1:2, DH * b:DH * b + DH] = delta
        dqpa[...] = jnp.zeros_like(dqpa)

        @pl.loop(0, 4)
        def _(i):
            rows = at(UNIT * i, UNIT, UNIT)
            grid = [jnp.concatenate(causal(i, b, UNIT), axis=0) for b in range(2)]
            add = jnp.where(jnp.concatenate(grid, axis=1), 0.0, -jnp.inf)
            dq, dk, dv = terms(
                kpb[0, rows, :], kpb[1, rows, :], qpb[...].reshape(UNIT, DH), dopb[...].reshape(UNIT, DH),
                rows_p[0:1, :], rows_p[1:2, :], add,
            )
            dqpa[...] += dq
            dacc[i, 0] += dk
            dacc[i, 1] += dv

    @pl.loop(0, 8)
    def _(t):
        i = (x + 1 + t) % 4
        ch = t // 4

        @pl.when(t % 4 == 0)
        def _():
            @pl.loop(0, 2)
            def _(b):
                q1(2 * (1 - y) + b, g, ch).wait_recv()
                do1(2 * (1 - y) + b, g, ch).wait_recv()

        unit_chunk(kpb, i, 1 - y, ch)

        @pl.when(t >= 4)
        def _():
            finish(psend, prx, pps, ppr, i)

    def dqp_copy(j):
        return remote(dqp_st.at[j], dqp_out, dps.at[j], dpr.at[0], prompt=mate(j))

    own_dqp = pltpu.make_async_copy(dqp_st.at[g], dqp_out, loc.at[4])

    @pl.when(g == handler)
    def _():
        dqp_st[...] = (dqpa[...] * SCALE).astype(BF16).reshape(4, ROWS, DH)
        own_dqp.start()

        @pl.loop(1, 4)
        def _(o):
            dqp_copy((g + o) % 4).start()

    def r_copy(src, dst):
        return remote(rst.at[dst], rrcv.at[src], rss, rsr, reply=dst)

    def all_r(count):
        pieces = pl.ds(0, count)
        return remote(rst.at[pieces], rrcv.at[pieces], rss, rsr, reply=(r + 1) % 32)

    def final_piece(kv, i, j):
        return dkvp_out.at[kv, at(16 * i, 16, 16), group_cols(j)]

    def g_send(dst):
        piece = final_piece(r // 16, r % 4, g)
        return remote(ag_st, piece, ags, agr, prompt=mate(turn), reply=dst)

    def all_g_sent(count):
        pieces = pl.ds(0, count)
        return remote(rst.at[pieces], rrcv.at[pieces], ags, agr, prompt=mate(turn), reply=(r + 1) % 32)

    def all_g():
        return remote(dkvp_out, dkvp_out, ags, agr, prompt=mate(turn), reply=(r + 1) % 32)

    own_g = pltpu.make_async_copy(ag_st, final_piece(r // 16, r % 4, g), agr)

    def others():
        for far in (2, 1, 3, 0):
            for dz in (4, 3, 5, 2, 6, 1, 7, 0):
                if far or dz:
                    yield 8 * ((r // 8 + far) % 4) + (r + dz) % 8

    def sum_column():
        totals = totals_of(psend, prx, pps, ppr)
        for kv in range(2):
            for i in range(16):
                rst[16 * kv + i] = totals[kv][16 * i:16 * i + 16]

        for other in others():
            r_copy(r, other).start()

    def sum_replies():
        total = rst[r].astype(F32)
        rrcv[r] = jnp.zeros((16, DH), BF16)
        all_r(31).wait_recv()

        for i in range(32):
            total = total + rrcv[i].astype(F32)
        ag_st[...] = total.astype(BF16)

        @pl.when(turn == g)
        def _():
            own_g.start()

        @pl.when(turn != g)
        def _():
            g_send(r).start()

        for other in others():
            g_send(other).start()

    dacc[...] = jnp.zeros_like(dacc)

    def dq_copy(src, dst):
        return remote(dq_st.at[dst], dqr_out.at[0, :, head_cols(src)], os_.at[dst], or_.at[src], prompt=mate(dst))

    own_dq = pltpu.make_async_copy(dq_st.at[g], dqr_out.at[0, :, head_cols(g)], loc.at[0])

    def stage_dq(half):
        part = (dqa[half] * SCALE).astype(BF16)
        for h in range(8):
            for b in range(2):
                dq_st[2 * half + b, :, DH * h:DH * h + DH] = part[HALF * h + ROWS * b:HALF * h + ROWS * b + ROWS]

    def send_near():
        stage_dq(y)
        own_dq.start()
        dq_copy(g, near).start()

    def send_far():
        stage_dq(1 - y)

        @pl.loop(0, 2)
        def _(b):
            dq_copy(g, 2 * (1 - y) + (c + b) % 2).start()

    ahead = (y == 1) | (x == 3)

    @pl.loop(0, 2)
    def _(stage):
        @pl.when((stage + y) % 2 == 1)
        def _():
            @pl.loop(0, 4)
            def _(i):
                @pl.when((stage == 0) & (i != x))
                def _():
                    kr2(i, x).wait_recv()
                    mk2(i, x).wait_recv()

                @pl.when((stage == 1) & (i > x))
                def _():
                    kr2(i, x).wait_recv()
                    mk2(i, x).wait_recv()

                half = (i + 3 - x) // 4
                set_bias(i, half, HALF)
                unit(krb, i, half, HALF, True)

                @pl.when((i > x) | (stage == 1))
                def _():
                    finish(rsend, rrx, rps, rpr, i)

                @pl.when((stage == 0) & (i == 2))
                def _():
                    sum_column()

        @pl.when((stage + y) % 2 == 0)
        def _():
            @pl.loop(0, x + 1)
            def _(i):
                @pl.when((stage == 0) & (i != x))
                def _():
                    kr2(i, x).wait_recv()
                    mk2(i, x).wait_recv()

                set_bias(i, 1, UNIT)
                unit(krb, i, 1, UNIT, True)

                @pl.when(stage == 1)
                def _():
                    finish(rsend, rrx, rps, rpr, i)

                @pl.when((stage == 0) & (i == (x + 2) // 3))
                def _():
                    sum_column()

        @pl.when((stage == 0) & ahead)
        def _():
            send_far()

    @pl.when((y == 0) & (x != 3))
    def _():
        send_far()

    sum_replies()
    send_near()

    totals = totals_of(rsend, rrx, rps, rpr)
    for kv in range(2):
        for j in range(4):
            dkv_st[j, kv] = totals[kv][ROWS * j:ROWS * j + ROWS]

    def f_copy(src, dst):
        return remote(dkv_st.at[dst], dkvr_out.at[:, 0, :, group_cols(src)], fs.at[dst], fr.at[src], prompt=mate(dst))

    own_f = pltpu.make_async_copy(dkv_st.at[g], dkvr_out.at[:, 0, :, group_cols(g)], loc.at[1])
    own_f.start()

    @pl.loop(1, 4)
    def _(o):
        f_copy(g, (g + o) % 4).start()

    @pl.when(g == handler)
    def _():
        own_dqp.wait()

        @pl.loop(1, 4)
        def _(o):
            dqp_copy((g + o) % 4).wait_send()

    @pl.when(g != handler)
    def _():
        own_qp.wait()
        own_dop.wait()
        for copy in hand(g):
            copy.wait_send()

    @pl.loop(1, 4)
    def _(o):
        other = (g + o) % 4
        kp1(g, other).wait_send()
        kr1(g, other).wait_send()
        mk1(g, other).wait_send()
        for ch in range(2):
            q1(g, other, ch).wait_send()
            do1(g, other, ch).wait_send()
        ls1(g, other).wait_send()
        ring = (x + o) % 4
        kp2(x, ring).wait_send()
        kr2(x, ring).wait_send()
        mk2(x, ring).wait_send()
        partial(psend, prx, pps, ppr, x, ring).wait_send()
        partial(rsend, rrx, rps, rpr, x, ring).wait_send()

    all_r(31).wait_send()

    @pl.when(turn == g)
    def _():
        all_g_sent(31).wait_send()

    @pl.when(turn != g)
    def _():
        all_g_sent(32).wait_send()

    @pl.loop(1, 4)
    def _(o):
        dq_copy(g, (g + o) % 4).wait_send()
        f_copy(g, (g + o) % 4).wait_send()

    own_dq.wait()
    own_f.wait()

    @pl.when(g != handler)
    def _():
        dqp_copy(g).wait_recv()

    @pl.loop(1, 4)
    def _(o):
        dq_copy((g + o) % 4, g).wait_recv()
        f_copy((g + o) % 4, g).wait_recv()

    all_g().wait_recv()


def call(*args):
    anywhere = pl.BlockSpec(memory_space=pl.ANY)
    vmem = pl.BlockSpec(memory_space=pltpu.VMEM)
    dma = pltpu.SemaphoreType.DMA
    out = jax.ShapeDtypeStruct
    four = [dma((4,))] * 2
    pairs = [dma((4, 2))] * 2
    results = pl.pallas_call(
        kernel,
        out_shape=(
            pltpu.VMEM((ROWS, DH), BF16),
            pltpu.VMEM((2, ROWS, 512), BF16),
            pltpu.VMEM((1, ROWS, 4096), BF16),
            pltpu.VMEM((2, 1, ROWS, 512), BF16),
        ),
        in_specs=[
            anywhere,
        ] * 12,
        out_specs=(vmem, vmem, vmem, vmem),
        scratch_shapes=[
            pltpu.VMEM((1, ROWS), F32),
            pltpu.VMEM((1, ROWS), F32),
            pltpu.VMEM((1, 32, ROWS), F32),
            pltpu.VMEM((1, 32, ROWS), F32),
            pltpu.SMEM((1,), jnp.int32),
            pltpu.VMEM((1, ROWS), jnp.int32),
            pltpu.VMEM((2, HALF, WIDE), BF16),
            pltpu.VMEM((2, HALF, WIDE), BF16),
            pltpu.VMEM((2, HALF, DH), BF16),
            pltpu.VMEM((2, HALF, DH), BF16),
            pltpu.VMEM((2, 1024, DH), BF16),
            pltpu.VMEM((2, 1024, DH), BF16),
            pltpu.VMEM((4, 2, 8, 128), F32),
            pltpu.VMEM((4, 2, 8, 128), F32),
            pltpu.VMEM((4, 8, 128), F32),
            pltpu.VMEM((4, 4, 8, 128), F32),
            pltpu.VMEM((2, 2, 1, 512), F32),
            pltpu.VMEM((2, 2, 1, 512), F32),
            pltpu.VMEM((8, UNIT), F32),
            pltpu.VMEM((UNIT, HALF), F32),
            pltpu.VMEM((2, WIDE, DH), F32),
            pltpu.VMEM((UNIT, DH), F32),
            pltpu.VMEM((4, 2, UNIT, DH), F32),
            pltpu.VMEM((2, UNIT, DH), F32),
            pltpu.VMEM((4, 2, UNIT, DH), BF16),
            pltpu.VMEM((4, 2, UNIT, DH), BF16),
            pltpu.VMEM((4, 2, UNIT, DH), BF16),
            pltpu.VMEM((4, 2, UNIT, DH), BF16),
            pltpu.VMEM((32, 16, DH), BF16),
            pltpu.VMEM((32, 16, DH), BF16),
            pltpu.VMEM((16, DH), BF16),
            pltpu.VMEM((4, ROWS, WIDE), BF16),
            pltpu.VMEM((4, ROWS, DH), BF16),
            pltpu.VMEM((4, 2, ROWS, DH), BF16),
            dma((14,)),
            *pairs,
            *pairs,
            *four,
            dma((3,)),
            dma((3, 4)),
            *four,
            *four,
            *four,
            *four,
            *four,
            *four,
            *four,
            *four,
            dma, dma,
            dma, dma,
            *four,
            *four,
            *four,
        ],
        compiler_params=pltpu.CompilerParams(
            collective_id=0, has_side_effects=True, vmem_limit_bytes=VMEM_LIMIT
        ),
    )(*args)

    def hand_over(*refs):
        sems = refs[-1]
        copies = [pltpu.make_async_copy(refs[i], refs[4 + i], sems.at[i]) for i in range(4)]
        for copy in copies:
            copy.start()
        for copy in copies:
            copy.wait()

    return pl.pallas_call(
        hand_over,
        out_shape=[out(a.shape, a.dtype) for a in results],
        in_specs=[anywhere] * 4,
        out_specs=[anywhere] * 4,
        scratch_shapes=[dma((4,))],
        compiler_params=pltpu.CompilerParams(vmem_limit_bytes=2**20),
    )(*results)


VMEM_LIMIT = 62 * 2**20


def solution(mesh):
    placed = (
        P("prompt", "reply"),
        P("prompt", "reply"),
        P(None, "prompt", None),
        P("reply", "prompt"),
        P("reply", "prompt"),
        P("reply", "prompt", None),
        P("reply", "prompt", None),
        P(None, "reply", "prompt", None),
        P("reply", None, "prompt"),
        P("reply", None, "prompt"),
        P("reply"),
        P("reply", "prompt"),
    )
    return jax.shard_map(
        call,
        mesh=mesh,
        in_specs=placed,
        out_specs=(
            P("prompt", "reply"),
            P(None, "prompt", None),
            P("reply", "prompt", None),
            P(None, "reply", "prompt", None),
        ),
        check_vma=False,
    )
```

```python
import jax
import jax.numpy as jnp
from jax import lax
from jax.experimental import pallas as pl
from jax.experimental.pallas import tpu as pltpu
from jax.sharding import PartitionSpec as P

MESH = pl.DeviceIdType.MESH
F32 = jnp.float32
BF16 = jnp.bfloat16
DH = 128
ROWS = 64
HALF = 128
UNIT = 256
WIDE = 1024
SCALE = DH**-0.5
LOG2E = 1.4426950408889634
NN = (((1,), (0,)), ((), ()))
NT = (((1,), (1,)), ((), ()))
TN = (((0,), (0,)), ((), ()))


def dot(a, b, dims=NN):
    return lax.dot_general(a, b, dims, preferred_element_type=F32)


def mod(a, n):
    return lax.rem(a, n)


def div(a, n):
    return lax.div(a, n)


def at(start, size, step):
    return pl.ds(pl.multiple_of(start, step), size)


def kernel(
    qp, dop, kvp, lsep_in, delp_in, qr, dor, kvr, lser_in, delr_in, rlen_in, rmask_in,
    dqp_out, dkvp_out, dqr_out, dkvr_out,
    lsep, delp, lser, delr, rlen, rmask, qbuf, dobuf, qpb, dopb, kpb, krb, lsd_st, lsd_rx, lsp_rx, msk, lse2, del2, rows_p, bias,
    dqa, dqpa, dacc, keep, psend, prx, rsend, rrx, rst, rrcv, ag_st, dq_st, dqp_st, dkv_st,
    loc, qs, qrx, ds, drx, ls, lrx, ps, prs, kp1s, kp1r, kr1s, kr1r, ms1, mr1, kp2s, kp2r, kr2s, kr2r, ms2, mr2,
    pps, ppr, rps, rpr, rss, rsr, ags, agr, os_, or_, fs, fr, dps, dpr,
):
    p = lax.axis_index("prompt")
    r = lax.axis_index("reply")
    y = div(p, 8)
    x = mod(div(p, 2), 4)
    c = mod(p, 2)
    g = 2 * y + c
    yh = div(r, 8)
    z = mod(r, 8)
    handler = yh
    turn = mod(div(r, 4), 4)
    beyond = 8 * mod(yh + 2 * y + 3, 4) + z
    near = 2 * y + 1 - c

    def device(i, j):
        if isinstance(j, int):
            return 8 * (j // 2) + 2 * i + j % 2
        return 8 * div(j, 2) + 2 * i + mod(j, 2)

    def mate(j):
        return device(x, j)

    def along(i):
        return 8 * y + 2 * i + c

    def remote(src, dst, send, recv, **where):
        return pltpu.make_async_remote_copy(
            src_ref=src, dst_ref=dst, send_sem=send, recv_sem=recv, device_id=where, device_id_type=MESH
        )

    barrier = pltpu.get_barrier_semaphore()

    def greet(**where):
        pl.semaphore_signal(barrier, inc=1, device_id=where, device_id_type=MESH)

    @pl.loop(1, 4)
    def _(o):
        greet(prompt=mate(mod(g + o, 4)))
        greet(prompt=along(mod(x + o, 4)))

    @pl.loop(0, 2)
    def _(b):
        greet(prompt=mate(2 * (1 - y) + b), reply=beyond)

    for o in range(1, 32):
        greet(reply=mod(r + o, 32))

    for o in range(1, 4):
        for i in range(8):
            greet(prompt=mate(mod(g + o, 4)), reply=16 * (i // 4) + 4 * g + i % 4)

    small = [
        pltpu.make_async_copy(src, dst, loc.at[8 + i])
        for i, (src, dst) in enumerate(
            ((lser_in, lser), (delr_in, delr), (lsep_in, lsep), (delp_in, delp), (rlen_in, rlen), (rmask_in, rmask))
        )
    ]
    for copy in small:
        copy.start()

    def group_cols(j):
        return at(DH * j, DH, DH)

    def head_cols(j):
        return at(WIDE * j, WIDE, WIDE)

    def seat(ref, j):
        return ref.at[div(j, 2), at(ROWS * mod(j, 2), ROWS, ROWS), :]

    def rows_at(ref, i, j):
        return ref.at[:, at(UNIT * i + ROWS * j, ROWS, ROWS), :]

    def unit_at(ref, i):
        return ref.at[:, at(UNIT * i, UNIT, UNIT), :]

    own_kp = pltpu.make_async_copy(kvp.at[:, :, group_cols(g)], rows_at(kpb, x, g), loc.at[2])
    own_kr = pltpu.make_async_copy(kvr.at[:, 0, :, group_cols(g)], rows_at(krb, x, g), loc.at[3])
    own_q = pltpu.make_async_copy(qr.at[0, :, head_cols(g)], seat(qbuf, g), loc.at[0])
    own_do = pltpu.make_async_copy(dor.at[0, :, head_cols(g)], seat(dobuf, g), loc.at[1])
    own_qp = pltpu.make_async_copy(qp, seat(qpb, g), loc.at[4])
    own_dop = pltpu.make_async_copy(dop, seat(dopb, g), loc.at[5])
    for copy in (own_kp, own_q, own_do, own_kr, own_qp, own_dop):
        copy.start()

    def twice(v):
        return jnp.concatenate([v, v], axis=1)

    for copy in small:
        copy.wait()

    for j in range(4):
        lsd_st[j, 0] = twice(lser[0, 8 * j:8 * j + 8, :])
        lsd_st[j, 1] = twice(delr[0, 8 * j:8 * j + 8, :])
    lsp_rx[g, 0:1, :] = twice(lsep[...])
    lsp_rx[g, 1:2, :] = twice(delp[...])
    lsp_rx[g, 2:8, :] = jnp.zeros((6, 128), F32)
    msk[x, g] = jnp.broadcast_to(twice(rmask[...].astype(F32)), (8, 128))
    lsd_rx[g] = lsd_st[g]

    @pl.when(turn == g)
    def _():
        pl.semaphore_wait(barrier, 3 + 3 + 2 + 31)

    @pl.when(turn != g)
    def _():
        pl.semaphore_wait(barrier, 3 + 3 + 2 + 31 + 32)

    def kp1(src, dst, **where):
        piece = kvp.at[:, :, group_cols(dst)]
        return remote(piece, rows_at(kpb, x, src), kp1s.at[dst], kp1r.at[src], prompt=mate(dst), **where)

    def kr1(src, dst):
        return remote(kvr.at[:, 0, :, group_cols(dst)], rows_at(krb, x, src), kr1s.at[dst], kr1r.at[src], prompt=mate(dst))

    def mk1(src, dst):
        return remote(msk.at[x, src], msk.at[x, src], ms1.at[dst], mr1.at[src], prompt=mate(dst))

    def chunk(ref, j, ch):
        return ref.at[div(j, 2), at(ROWS * mod(j, 2), ROWS, ROWS), at(512 * ch, 512, 512)]

    def q1(src, dst, ch):
        piece = qr.at[0, :, at(WIDE * dst + 512 * ch, 512, 512)]
        return remote(piece, chunk(qbuf, src, ch), qs.at[dst, ch], qrx.at[src, ch], prompt=mate(dst))

    def do1(src, dst, ch):
        piece = dor.at[0, :, at(WIDE * dst + 512 * ch, 512, 512)]
        return remote(piece, chunk(dobuf, src, ch), ds.at[dst, ch], drx.at[src, ch], prompt=mate(dst))

    def ls1(src, dst):
        return remote(lsd_st.at[dst], lsd_rx.at[src], ls.at[dst], lrx.at[src], prompt=mate(dst))

    def hand(src):
        return [
            remote(qp, seat(qpb, src), ps.at[0], prs.at[0, src], prompt=mate(handler)),
            remote(dop, seat(dopb, src), ps.at[1], prs.at[1, src], prompt=mate(handler)),
            remote(lsp_rx.at[src], lsp_rx.at[src], ps.at[2], prs.at[2, src], prompt=mate(handler)),
        ]

    @pl.loop(0, 2)
    def _(b):
        kp1(g, 2 * (1 - y) + mod(c + b, 2), reply=beyond).start()

    kp1(g, near).start()

    ls1(g, near).start()
    for ch in range(2):
        q1(g, near, ch).start()
        do1(g, near, ch).start()

    @pl.loop(0, 2)
    def _(b):
        far = 2 * (1 - y) + mod(c + b, 2)
        ls1(g, far).start()
        kr1(g, far).start()
        mk1(g, far).start()

    kr1(g, near).start()
    mk1(g, near).start()

    @pl.when(g != handler)
    def _():
        for copy in hand(g):
            copy.start()

    @pl.loop(0, 4)
    def _(b):
        far = 2 * (1 - y) + mod(c + b, 2)
        q1(g, far, div(b, 2)).start()
        do1(g, far, div(b, 2)).start()

    def kp2(src, dst):
        return remote(unit_at(kpb, src), unit_at(kpb, src), kp2s.at[dst], kp2r.at[src], prompt=along(dst))

    def kr2(src, dst):
        return remote(unit_at(krb, src), unit_at(krb, src), kr2s.at[dst], kr2r.at[src], prompt=along(dst))

    def mk2(src, dst):
        return remote(msk.at[src], msk.at[src], ms2.at[dst], mr2.at[src], prompt=along(dst))

    own_kp.wait()

    @pl.loop(1, 4)
    def _(o):
        kp1(mod(g + o, 4), g).wait_recv()

    @pl.loop(1, 4)
    def _(o):
        kp2(x, mod(x + 4 - o, 4)).start()

    dqa[...] = jnp.zeros_like(dqa)
    dacc[...] = jnp.zeros_like(dacc)

    def pass_reply_keys():
        own_kr.wait()

        @pl.loop(1, 4)
        def _(o):
            kr1(mod(g + o, 4), g).wait_recv()
            mk1(mod(g + o, 4), g).wait_recv()

        @pl.loop(1, 4)
        def _(o):
            kr2(x, mod(x + 4 - o, 4)).start()
            mk2(x, mod(x + 4 - o, 4)).start()

    pass_reply_keys()

    lane = lax.broadcasted_iota(jnp.int32, (1, 128), 1)
    first = lane < 64

    def rows_of(half):
        alive = HALF * x + 512 * half + lane < rlen[0]
        lse = jnp.where(first, lsd_rx[2 * half, 0], lsd_rx[2 * half + 1, 0]) * LOG2E
        lse = jnp.where(alive, lse, jnp.inf)
        delta = jnp.where(first, lsd_rx[2 * half, 1], lsd_rx[2 * half + 1, 1])
        for ch in range(2):
            lse2[half, ch] = jnp.concatenate([lse[h:h + 1] for h in range(4 * ch, 4 * ch + 4)], axis=1)
            del2[half, ch] = jnp.concatenate([delta[h:h + 1] for h in range(4 * ch, 4 * ch + 4)], axis=1)

    own_q.wait()
    own_do.wait()
    for ch in range(2):
        q1(near, g, ch).wait_recv()
        do1(near, g, ch).wait_recv()
    ls1(near, g).wait_recv()
    rows_of(y)

    def heads(ref, half):
        return jnp.concatenate([ref[half, :, DH * h:DH * h + DH] for h in range(8)], axis=0)

    def terms(keys, vals, q, do, lse_row, del_row, add):
        score = dot(keys, q, NT) * (SCALE * LOG2E) - lse_row
        if add is not None:
            score = score + add
        prob = jnp.exp2(score)
        dprob = dot(vals, do, NT)
        prob_b = prob.astype(BF16)
        ds_b = (prob * (dprob - del_row)).astype(BF16)
        return dot(ds_b, keys, TN), dot(ds_b, q), dot(prob_b, do)

    def both(ref, half):
        return jnp.concatenate([ref[half, 0], ref[half, 1]], axis=1)

    def unit(ref, i, half, size, masked):
        rows = at(UNIT * i, size, UNIT)
        add = None
        if masked:
            add = jnp.concatenate([bias[0:size, :]] * 8, axis=1)
        dq, dk, dv = terms(
            ref[0, rows, :], ref[1, rows, :], heads(qbuf, half), heads(dobuf, half), both(lse2, half), both(del2, half), add
        )
        dqa[half] += dq
        dacc[i, 0, 0:size, :] += dk
        dacc[i, 1, 0:size, :] += dv

    def four(ref, half, ch):
        return jnp.concatenate([ref[half, :, at(512 * ch + DH * h, DH, DH)] for h in range(4)], axis=0)

    def unit_chunk(ref, i, half, ch):
        rows = at(UNIT * i, UNIT, UNIT)
        dq, dk, dv = terms(
            ref[0, rows, :], ref[1, rows, :], four(qbuf, half, ch), four(dobuf, half, ch), lse2[half, ch], del2[half, ch], None
        )
        dqa[half, at(512 * ch, 512, 512), :] += dq
        dacc[i, 0] += dk
        dacc[i, 1] += dv

    def causal(i, half, size):
        key = lax.broadcasted_iota(jnp.int32, (HALF, HALF), 0)
        query = lax.broadcasted_iota(jnp.int32, (HALF, HALF), 1)
        return [key - query <= HALF * x + 512 * half - HALF * i - 512 * b for b in range(size // HALF)]

    def set_bias(i, half, size):
        for b, ok in enumerate(causal(i, half, size)):
            row = jnp.where(first, msk[i, 2 * b, 0:1, :], msk[i, 2 * b + 1, 0:1, :])
            column = jnp.transpose(jnp.broadcast_to(row, (HALF, HALF)))
            bias[HALF * b:HALF * b + HALF, :] = jnp.where(ok & (column > 0.5), 0.0, -jnp.inf)

    def partial(buf, rx, send, recv, src, dst):
        return remote(buf.at[dst], rx.at[src], send.at[dst], recv.at[src], prompt=along(dst))

    def finish(buf, rx, send, recv, i):
        @pl.when(i == x)
        def _():
            keep[0] = dacc[x, 0] * SCALE
            keep[1] = dacc[x, 1]

        @pl.when(i != x)
        def _():
            buf[i, 0] = (dacc[i, 0] * SCALE).astype(BF16)
            buf[i, 1] = dacc[i, 1].astype(BF16)
            partial(buf, rx, send, recv, x, i).start()

    def totals_of(buf, rx, send, recv):
        @pl.loop(1, 4)
        def _(o):
            partial(buf, rx, send, recv, mod(x + o, 4), x).wait_recv()

        totals = []
        for kv in range(2):
            total = keep[kv]
            for o in range(1, 4):
                total = total + rx[mod(x + o, 4), kv].astype(F32)
            totals.append(total.astype(BF16))
        return totals

    @pl.loop(0, 4)
    def _(t):
        i = mod(x + t, 4)

        @pl.when(t > 0)
        def _():
            kp2(i, x).wait_recv()

        unit(kpb, i, y, UNIT, False)

    @pl.loop(0, 2)
    def _(b):
        ls1(2 * (1 - y) + b, g).wait_recv()

    rows_of(1 - y)

    @pl.when(g == handler)
    def _():
        own_qp.wait()
        own_dop.wait()

        @pl.loop(1, 4)
        def _(o):
            for copy in hand(mod(g + o, 4)):
                copy.wait_recv()

        for b in range(2):
            lse = jnp.where(first, lsp_rx[2 * b, 0:1, :], lsp_rx[2 * b + 1, 0:1, :]) * LOG2E
            delta = jnp.where(first, lsp_rx[2 * b, 1:2, :], lsp_rx[2 * b + 1, 1:2, :])
            rows_p[0:1, DH * b:DH * b + DH] = lse
            rows_p[1:2, DH * b:DH * b + DH] = delta
        dqpa[...] = jnp.zeros_like(dqpa)

        @pl.loop(0, 4)
        def _(i):
            rows = at(UNIT * i, UNIT, UNIT)
            grid = [jnp.concatenate(causal(i, b, UNIT), axis=0) for b in range(2)]
            add = jnp.where(jnp.concatenate(grid, axis=1), 0.0, -jnp.inf)
            dq, dk, dv = terms(
                kpb[0, rows, :], kpb[1, rows, :], qpb[...].reshape(UNIT, DH), dopb[...].reshape(UNIT, DH),
                rows_p[0:1, :], rows_p[1:2, :], add,
            )
            dqpa[...] += dq
            dacc[i, 0] += dk
            dacc[i, 1] += dv

    @pl.loop(0, 8)
    def _(t):
        i = mod(x + 1 + t, 4)
        ch = div(t, 4)

        @pl.when(mod(t, 4) == 0)
        def _():
            @pl.loop(0, 2)
            def _(b):
                q1(2 * (1 - y) + b, g, ch).wait_recv()
                do1(2 * (1 - y) + b, g, ch).wait_recv()

        unit_chunk(kpb, i, 1 - y, ch)

        @pl.when(t >= 4)
        def _():
            finish(psend, prx, pps, ppr, i)

    def dqp_copy(j):
        return remote(dqp_st.at[j], dqp_out, dps.at[j], dpr.at[0], prompt=mate(j))

    own_dqp = pltpu.make_async_copy(dqp_st.at[g], dqp_out, loc.at[4])

    @pl.when(g == handler)
    def _():
        dqp_st[...] = (dqpa[...] * SCALE).astype(BF16).reshape(4, ROWS, DH)
        own_dqp.start()

        @pl.loop(1, 4)
        def _(o):
            dqp_copy(mod(g + o, 4)).start()

    def r_copy(src, dst):
        return remote(rst.at[dst], rrcv.at[src], rss, rsr, reply=dst)

    def all_r(count):
        pieces = pl.ds(0, count)
        return remote(rst.at[pieces], rrcv.at[pieces], rss, rsr, reply=mod(r + 1, 32))

    def final_piece(kv, i, j):
        return dkvp_out.at[kv, at(16 * i, 16, 16), group_cols(j)]

    def g_send(dst):
        piece = final_piece(div(r, 16), mod(r, 4), g)
        return remote(ag_st, piece, ags, agr, prompt=mate(turn), reply=dst)

    def all_g_sent(count):
        pieces = pl.ds(0, count)
        return remote(rst.at[pieces], rrcv.at[pieces], ags, agr, prompt=mate(turn), reply=mod(r + 1, 32))

    def all_g():
        return remote(dkvp_out, dkvp_out, ags, agr, prompt=mate(turn), reply=mod(r + 1, 32))

    own_g = pltpu.make_async_copy(ag_st, final_piece(div(r, 16), mod(r, 4), g), agr)

    def others():
        for far in (2, 1, 3, 0):
            for dz in (4, 3, 5, 2, 6, 1, 7, 0):
                if far or dz:
                    yield 8 * mod(yh + far, 4) + mod(z + dz, 8)

    def sum_column():
        totals = totals_of(psend, prx, pps, ppr)
        for kv in range(2):
            for i in range(16):
                rst[16 * kv + i] = totals[kv][16 * i:16 * i + 16]

        for other in others():
            r_copy(r, other).start()

    def sum_replies():
        total = rst[r].astype(F32)
        rrcv[r] = jnp.zeros((16, DH), BF16)
        all_r(31).wait_recv()

        for i in range(32):
            total = total + rrcv[i].astype(F32)
        ag_st[...] = total.astype(BF16)

        @pl.when(turn == g)
        def _():
            own_g.start()

        @pl.when(turn != g)
        def _():
            g_send(r).start()

        for other in others():
            g_send(other).start()

    dacc[...] = jnp.zeros_like(dacc)

    def dq_copy(src, dst):
        return remote(dq_st.at[dst], dqr_out.at[0, :, head_cols(src)], os_.at[dst], or_.at[src], prompt=mate(dst))

    own_dq = pltpu.make_async_copy(dq_st.at[g], dqr_out.at[0, :, head_cols(g)], loc.at[0])

    def stage_dq(half):
        part = (dqa[half] * SCALE).astype(BF16)
        for h in range(8):
            for b in range(2):
                dq_st[2 * half + b, :, DH * h:DH * h + DH] = part[HALF * h + ROWS * b:HALF * h + ROWS * b + ROWS]

    def send_near():
        stage_dq(y)
        own_dq.start()
        dq_copy(g, near).start()

    def send_far():
        stage_dq(1 - y)

        @pl.loop(0, 2)
        def _(b):
            dq_copy(g, 2 * (1 - y) + mod(c + b, 2)).start()

    ahead = (y == 1) | (x == 3)

    @pl.loop(0, 2)
    def _(stage):
        @pl.when((stage + y) % 2 == 1)
        def _():
            @pl.loop(0, 4)
            def _(i):
                @pl.when((stage == 0) & (i != x))
                def _():
                    kr2(i, x).wait_recv()
                    mk2(i, x).wait_recv()

                @pl.when((stage == 1) & (i > x))
                def _():
                    kr2(i, x).wait_recv()
                    mk2(i, x).wait_recv()

                half = (i + 3 - x) // 4
                set_bias(i, half, HALF)
                unit(krb, i, half, HALF, True)

                @pl.when((i > x) | (stage == 1))
                def _():
                    finish(rsend, rrx, rps, rpr, i)

                @pl.when((stage == 0) & (i == 2))
                def _():
                    sum_column()

        @pl.when((stage + y) % 2 == 0)
        def _():
            @pl.loop(0, x + 1)
            def _(i):
                @pl.when((stage == 0) & (i != x))
                def _():
                    kr2(i, x).wait_recv()
                    mk2(i, x).wait_recv()

                set_bias(i, 1, UNIT)
                unit(krb, i, 1, UNIT, True)

                @pl.when(stage == 1)
                def _():
                    finish(rsend, rrx, rps, rpr, i)

                @pl.when((stage == 0) & (i == (x + 2) // 3))
                def _():
                    sum_column()

        @pl.when((stage == 0) & ahead)
        def _():
            send_far()

    @pl.when((y == 0) & (x != 3))
    def _():
        send_far()

    sum_replies()
    send_near()

    totals = totals_of(rsend, rrx, rps, rpr)
    for kv in range(2):
        for j in range(4):
            dkv_st[j, kv] = totals[kv][ROWS * j:ROWS * j + ROWS]

    def f_copy(src, dst):
        return remote(dkv_st.at[dst], dkvr_out.at[:, 0, :, group_cols(src)], fs.at[dst], fr.at[src], prompt=mate(dst))

    own_f = pltpu.make_async_copy(dkv_st.at[g], dkvr_out.at[:, 0, :, group_cols(g)], loc.at[1])
    own_f.start()

    @pl.loop(1, 4)
    def _(o):
        f_copy(g, mod(g + o, 4)).start()

    @pl.when(g == handler)
    def _():
        own_dqp.wait()

        @pl.loop(1, 4)
        def _(o):
            dqp_copy(mod(g + o, 4)).wait_send()

    @pl.when(g != handler)
    def _():
        own_qp.wait()
        own_dop.wait()
        for copy in hand(g):
            copy.wait_send()

    @pl.loop(1, 4)
    def _(o):
        other = mod(g + o, 4)
        kp1(g, other).wait_send()
        kr1(g, other).wait_send()
        mk1(g, other).wait_send()
        for ch in range(2):
            q1(g, other, ch).wait_send()
            do1(g, other, ch).wait_send()
        ls1(g, other).wait_send()
        ring = mod(x + o, 4)
        kp2(x, ring).wait_send()
        kr2(x, ring).wait_send()
        mk2(x, ring).wait_send()
        partial(psend, prx, pps, ppr, x, ring).wait_send()
        partial(rsend, rrx, rps, rpr, x, ring).wait_send()

    all_r(31).wait_send()

    @pl.when(turn == g)
    def _():
        all_g_sent(31).wait_send()

    @pl.when(turn != g)
    def _():
        all_g_sent(32).wait_send()

    @pl.loop(1, 4)
    def _(o):
        dq_copy(g, mod(g + o, 4)).wait_send()
        f_copy(g, mod(g + o, 4)).wait_send()

    own_dq.wait()
    own_f.wait()

    @pl.when(g != handler)
    def _():
        dqp_copy(g).wait_recv()

    @pl.loop(1, 4)
    def _(o):
        dq_copy(mod(g + o, 4), g).wait_recv()
        f_copy(mod(g + o, 4), g).wait_recv()

    all_g().wait_recv()


def call(*args):
    anywhere = pl.BlockSpec(memory_space=pl.ANY)
    vmem = pl.BlockSpec(memory_space=pltpu.VMEM)
    dma = pltpu.SemaphoreType.DMA
    out = jax.ShapeDtypeStruct
    four = [dma((4,))] * 2
    pairs = [dma((4, 2))] * 2
    results = pl.pallas_call(
        kernel,
        out_shape=(
            pltpu.VMEM((ROWS, DH), BF16),
            pltpu.VMEM((2, ROWS, 512), BF16),
            pltpu.VMEM((1, ROWS, 4096), BF16),
            pltpu.VMEM((2, 1, ROWS, 512), BF16),
        ),
        in_specs=[
            anywhere,
        ] * 12,
        out_specs=(vmem, vmem, vmem, vmem),
        scratch_shapes=[
            pltpu.VMEM((1, ROWS), F32),
            pltpu.VMEM((1, ROWS), F32),
            pltpu.VMEM((1, 32, ROWS), F32),
            pltpu.VMEM((1, 32, ROWS), F32),
            pltpu.SMEM((1,), jnp.int32),
            pltpu.VMEM((1, ROWS), jnp.int32),
            pltpu.VMEM((2, HALF, WIDE), BF16),
            pltpu.VMEM((2, HALF, WIDE), BF16),
            pltpu.VMEM((2, HALF, DH), BF16),
            pltpu.VMEM((2, HALF, DH), BF16),
            pltpu.VMEM((2, 1024, DH), BF16),
            pltpu.VMEM((2, 1024, DH), BF16),
            pltpu.VMEM((4, 2, 8, 128), F32),
            pltpu.VMEM((4, 2, 8, 128), F32),
            pltpu.VMEM((4, 8, 128), F32),
            pltpu.VMEM((4, 4, 8, 128), F32),
            pltpu.VMEM((2, 2, 1, 512), F32),
            pltpu.VMEM((2, 2, 1, 512), F32),
            pltpu.VMEM((8, UNIT), F32),
            pltpu.VMEM((UNIT, HALF), F32),
            pltpu.VMEM((2, WIDE, DH), F32),
            pltpu.VMEM((UNIT, DH), F32),
            pltpu.VMEM((4, 2, UNIT, DH), F32),
            pltpu.VMEM((2, UNIT, DH), F32),
            pltpu.VMEM((4, 2, UNIT, DH), BF16),
            pltpu.VMEM((4, 2, UNIT, DH), BF16),
            pltpu.VMEM((4, 2, UNIT, DH), BF16),
            pltpu.VMEM((4, 2, UNIT, DH), BF16),
            pltpu.VMEM((32, 16, DH), BF16),
            pltpu.VMEM((32, 16, DH), BF16),
            pltpu.VMEM((16, DH), BF16),
            pltpu.VMEM((4, ROWS, WIDE), BF16),
            pltpu.VMEM((4, ROWS, DH), BF16),
            pltpu.VMEM((4, 2, ROWS, DH), BF16),
            dma((14,)),
            *pairs,
            *pairs,
            *four,
            dma((3,)),
            dma((3, 4)),
            *four,
            *four,
            *four,
            *four,
            *four,
            *four,
            *four,
            *four,
            dma, dma,
            dma, dma,
            *four,
            *four,
            *four,
        ],
        compiler_params=pltpu.CompilerParams(
            collective_id=0, has_side_effects=True, vmem_limit_bytes=VMEM_LIMIT
        ),
    )(*args)

    def hand_over(*refs):
        sems = refs[-1]
        copies = [pltpu.make_async_copy(refs[i], refs[4 + i], sems.at[i]) for i in range(4)]
        for copy in copies:
            copy.start()
        for copy in copies:
            copy.wait()

    return pl.pallas_call(
        hand_over,
        out_shape=[out(a.shape, a.dtype) for a in results],
        in_specs=[anywhere] * 4,
        out_specs=[anywhere] * 4,
        scratch_shapes=[dma((4,))],
        compiler_params=pltpu.CompilerParams(vmem_limit_bytes=2**20),
    )(*results)


VMEM_LIMIT = 62 * 2**20


def solution(mesh):
    placed = (
        P("prompt", "reply"),
        P("prompt", "reply"),
        P(None, "prompt", None),
        P("reply", "prompt"),
        P("reply", "prompt"),
        P("reply", "prompt", None),
        P("reply", "prompt", None),
        P(None, "reply", "prompt", None),
        P("reply", None, "prompt"),
        P("reply", None, "prompt"),
        P("reply"),
        P("reply", "prompt"),
    )
    return jax.shard_map(
        call,
        mesh=mesh,
        in_specs=placed,
        out_specs=(
            P("prompt", "reply"),
            P(None, "prompt", None),
            P("reply", "prompt", None),
            P(None, "reply", "prompt", None),
        ),
        check_vma=False,
    )
```
